128 devices in a mesh: pipe: 4 (over x_hi, core), expert: 32 (over x_lo, y, z).
Axes of the slice: x: 4 (x_hi: 2, x_lo: 2; x = x_hi * 2 + x_lo), y: 4, z: 4, core: 2. Of those that a mesh axis runs over, the one named last changes fastest.
Arguments:
- held_a: bfloat16 [4, 1024, 7168], P('pipe', 'expert'), may hold values from -6 to 6
- held_b: bfloat16 [4, 1024, 7168], P('pipe', 'expert'), may hold values from -6 to 6
- new_a: bfloat16 [1024, 7168], P('expert'), may hold values from -6 to 6
- new_b: bfloat16 [1024, 7168], P('expert'), may hold values from -6 to 6
- expert_ids: int32 [4, 4, 1024, 2], P('pipe', None, 'expert'), may hold values from 0 to 7, all different within a row; in each aligned block of 32 rows (0 to 31, 32 to 63, ..., all dimensions but the last counted through in order) at most 10 rows name the same one
- route_probs: float32 [4, 4, 1024, 2], P('pipe', None, 'expert'), may hold values from 0.1 to 1
- saved_gate_up: bfloat16 [4, 4, 320, 2, 8192], P('pipe', None, None, None, 'expert'), may hold values from -8 to 8
- w_gate: bfloat16 [4, 7168, 8192], P('pipe', None, 'expert'), may hold values from -0.0625 to 0.0625
- w_up: bfloat16 [4, 7168, 8192], P('pipe', None, 'expert'), may hold values from -0.0625 to 0.0625
- w_down: bfloat16 [4, 8192, 7168], P('pipe', 'expert'), may hold values from -0.1875 to 0.1875
Outputs:
- first_a: bfloat16 [4, 1024, 7168], P('pipe', 'expert')
- first_b: bfloat16 [4, 1024, 7168], P('pipe', 'expert')
- second_a: bfloat16 [4, 1024, 7168], P('pipe', 'expert')
- second_b: bfloat16 [4, 1024, 7168], P('pipe', 'expert')
The draws below stay inside these ranges and needn't reach their ends.
Inputs may be any that keep to these rules, and one draw needn't show every extreme that they name: `expert_ids`: in each aligned block of 32 tokens (one index of expert's tokens of one section and micro-batch) no expert is named by more than 10 tokens, a bound that some block reaches; each token names 2 different experts.
All inputs are finite; a program needn't handle non-finite values.
Results may differ from the reference program's by a relative error of at most 0.017.
Values may be sent and summed in bfloat16 or wider, within the bound.
A program may use at most 192 MiB of HBM per device.

```python
import math
import jax
import jax.numpy as jnp
import numpy as np
from jax import lax

D = 7168
HID = 1024
EXPERTS = 8
TOPK = 2
MICRO = 4
TOK_DEV = 32
TOKENS = 1024
CAP = 10
SLICES = 4
HID_DEV = 256
SLOTS = 320
N_PIPE = 4
N_EXPERT = 32


def level_of(stream_key, extent, pieces, least, largest):
    def one(dim, shards_of):
        steps = jax.random.uniform(jax.random.fold_in(jax.random.fold_in(stream_key, 6), dim), (shards_of,), jnp.float32, least / len(pieces), largest / len(pieces))
        return jnp.repeat(jnp.exp(steps), extent[dim] // shards_of).reshape((-1,) + (1,) * (len(extent) - dim - 1))

    factor_of = one(*pieces[0])
    for cut in pieces[1:]:
        factor_of = factor_of * one(*cut)
    return factor_of


def deal_out(rng, own, number, rows, amount, top, reach, lean):
    order = jax.random.permutation(rng, amount)
    crowded, ordinary = load_shares(amount, rows * top, reach, lean, True), load_shares(amount, rows * top, reach, lean, False)
    places = jnp.arange(amount)

    def named(sizes, turn):
        used = int((sizes > 0).sum())
        fixed = max(1, used // 4)
        moved = fixed + (places - fixed + turn * (used - fixed)) % max(1, amount - fixed)
        return jnp.zeros((amount,), jnp.int32).at[order[jnp.where(places < fixed, places, moved)]].set(jnp.asarray(sizes, jnp.int32))

    sizes = jnp.where(number % 4 == 0, named(crowded, number // 4), named(ordinary, number - number // 4 - 1))
    mixed = jax.random.permutation(jax.random.fold_in(own, 3), amount)
    donor, sink = mixed[0:amount // 2 * 2:2], mixed[1:amount // 2 * 2:2]
    room = jnp.minimum(sizes[donor] - 1, reach - sizes[sink]) // 2
    room = jnp.where((donor == order[0]) | (sink == order[0]) | (sizes[sink] == 0), 0, jnp.maximum(room, 0))
    moved = jax.random.randint(jax.random.fold_in(own, 4), (amount // 2,), 0, 1 << 20) % (room + 1)
    sizes = sizes.at[donor].add(-moved).at[sink].add(moved)
    labels = jnp.searchsorted(jnp.cumsum(sizes), jnp.arange(rows * top), side="right").astype(jnp.int32)
    table = labels.reshape(top, rows).T
    table = table[jax.random.permutation(jax.random.fold_in(own, 1), rows)]
    turn = jax.random.randint(jax.random.fold_in(own, 2), (rows, 1), 0, top)
    return jnp.take_along_axis(table, (jnp.arange(top)[None, :] + turn) % top, axis=1)


def load_shares(count, total, bound, lean, full):
    loads = [(1 << 20) // math.isqrt(standing ** lean) + 1 for standing in range(1, count + 1)]
    largest = bound if full else min(bound, max(-(-total // count), total * loads[0] // sum(loads)))
    least = 1 if total - largest >= count - 1 else 0
    holding, surplus = [largest] + [least] * (count - 1), total - largest - least * (count - 1)
    while surplus > 0:
        movable = [i for i in range(1, count) if holding[i] < largest] or [i for i in range(1, count) if holding[i] < bound]
        mass, budget = sum([loads[i] for i in movable]), surplus
        for i in movable:
            extra = min(bound - holding[i], max(1, budget * loads[i] // mass), surplus)
            holding[i] = holding[i] + extra
            surplus = surplus - extra
    return np.array(holding)


def normal_values(rng, dims, deviation, bound, pieces=(), kind=jnp.bfloat16):
    values = deviation * jax.random.normal(rng, dims, jnp.float32)
    if pieces:
        values = values * level_of(rng, dims, pieces, -0.22, 0.18)
    return jnp.clip(values, -bound, bound).astype(kind)


def setup_inputs(seed: int = 0) -> dict:
    seeds = jax.random.split(jax.random.key(seed), 11)
    held_a = normal_values(seeds[0], (N_PIPE, TOKENS, D), 1.0, 6.0, ((0, 4), (1, 32)))
    held_b = normal_values(seeds[1], (N_PIPE, TOKENS, D), 1.0, 6.0, ((0, 4), (1, 32)))
    new_a = normal_values(seeds[2], (TOKENS, D), 1.0, 6.0, ((0, 32),))
    new_b = normal_values(seeds[3], (TOKENS, D), 1.0, 6.0, ((0, 32),))
    expert_ids_keys = jax.random.split(jax.random.fold_in(seeds[4], 1), N_PIPE * MICRO * TOKENS // TOK_DEV)
    expert_ids_turns = jax.random.permutation(jax.random.fold_in(seeds[4], 3), N_PIPE * MICRO * TOKENS // TOK_DEV)
    expert_ids = jax.vmap(lambda own, number: deal_out(jax.random.fold_in(seeds[4], 2), own, number, TOK_DEV, EXPERTS, TOPK, CAP, 2))(expert_ids_keys, expert_ids_turns).reshape((N_PIPE, MICRO, TOKENS, TOPK))
    route_probs = jnp.clip(jnp.exp(math.log(1.0) - 2.3025851 * jax.random.uniform(seeds[5], (N_PIPE, MICRO, TOKENS, TOPK), jnp.float32) ** level_of(seeds[5], (N_PIPE, MICRO, TOKENS, TOPK), ((0, 4), (2, 32)), -0.2, 0.2)), 0.1, 1.0)
    saved_gate_up = normal_values(seeds[6], (N_PIPE, MICRO, SLOTS, 2, EXPERTS * HID), 1.5, 8.0, ((0, 4), (4, 32)))
    w_gate = normal_values(seeds[7], (N_PIPE, D, EXPERTS * HID), D ** -0.5, 0.0625, ((0, 4), (2, 32)))
    w_up = normal_values(seeds[8], (N_PIPE, D, EXPERTS * HID), D ** -0.5, 0.0625, ((0, 4), (2, 32)))
    w_down = normal_values(seeds[9], (N_PIPE, EXPERTS * HID, D), HID ** -0.5, 0.1875, ((0, 4), (1, 32)))
    return {"held_a": held_a, "held_b": held_b, "new_a": new_a, "new_b": new_b, "expert_ids": expert_ids, "route_probs": route_probs, "saved_gate_up": saved_gate_up, "w_gate": w_gate, "w_up": w_up, "w_down": w_down}


def layer(grads, route_ids, probs, saved, gate_w, up_w, down_w):
    total_rows = TOKENS * TOPK
    flat_ids = route_ids.reshape(-1).astype(jnp.int32)
    onehot = (flat_ids[:, None] == jnp.arange(EXPERTS, dtype=jnp.int32)[None, :]).astype(jnp.int32)
    per_block = onehot.reshape(N_EXPERT, TOK_DEV * TOPK, EXPERTS)
    ranking = jnp.sum((jnp.cumsum(per_block, axis=1) - 1) * per_block, axis=2).reshape(-1)
    blocks = jnp.arange(total_rows, dtype=jnp.int32) // (TOK_DEV * TOPK)
    target = (blocks * CAP + ranking).astype(jnp.int32)
    scaled = (grads.astype(jnp.float32)[:, None, :] * probs[:, :, None]).astype(jnp.bfloat16).reshape(total_rows, D)
    scaled_f = scaled.astype(jnp.float32)

    def one_expert(carry, expert):
        selected = flat_ids == expert
        where_to = jnp.where(selected, target, SLOTS).astype(jnp.int32)
        buffer = jnp.zeros((SLOTS, D), jnp.float32).at[where_to].add(scaled_f, mode="drop")
        start = (expert * HID).astype(jnp.int32)
        gate_pre = lax.dynamic_slice_in_dim(saved[:, 0, :], start, HID, 1).astype(jnp.float32)
        up_pre = lax.dynamic_slice_in_dim(saved[:, 1, :], start, HID, 1).astype(jnp.float32)
        down_rows = lax.dynamic_slice_in_dim(down_w, start, HID, 0).astype(jnp.float32)
        gate_cols = lax.dynamic_slice_in_dim(gate_w, start, HID, 1).astype(jnp.float32)
        up_cols = lax.dynamic_slice_in_dim(up_w, start, HID, 1).astype(jnp.float32)
        hidden_grad = jnp.dot(buffer, down_rows.T, preferred_element_type=jnp.float32)
        sigmoid_gate = jax.nn.sigmoid(gate_pre)
        gate_grad = (hidden_grad * up_pre * sigmoid_gate * (1.0 + gate_pre * (1.0 - sigmoid_gate))).astype(jnp.bfloat16)
        up_grad = (hidden_grad * gate_pre * sigmoid_gate).astype(jnp.bfloat16)
        gate_split = gate_grad.astype(jnp.float32).reshape(SLOTS, SLICES, HID_DEV)
        up_split = up_grad.astype(jnp.float32).reshape(SLOTS, SLICES, HID_DEV)
        parts = jnp.einsum("rjh,djh->jrd", gate_split, gate_cols.reshape(D, SLICES, HID_DEV))
        parts = parts + jnp.einsum("rjh,djh->jrd", up_split, up_cols.reshape(D, SLICES, HID_DEV))
        summed = jnp.sum(parts.astype(jnp.bfloat16).astype(jnp.float32), axis=0)
        picked = summed[jnp.minimum(where_to, SLOTS - 1)] * selected[:, None].astype(jnp.float32)
        return carry + picked, None

    total, unused = lax.scan(one_expert, jnp.zeros((total_rows, D), jnp.float32), jnp.arange(EXPERTS, dtype=jnp.int32))
    result = grads.astype(jnp.float32) + jnp.sum(total.reshape(TOKENS, TOPK, D), axis=1)
    return result.astype(jnp.bfloat16)


def section_layer(section, micro, grads, expert_ids, route_probs, saved_gate_up, w_gate, w_up, w_down):
    return layer(grads, expert_ids[section, micro], route_probs[section, micro], saved_gate_up[section, micro], w_gate[section], w_up[section], w_down[section])


def reference(held_a, held_b, new_a, new_b, expert_ids, route_probs, saved_gate_up, w_gate, w_up, w_down):
    shared = (expert_ids, route_probs, saved_gate_up, w_gate, w_up, w_down)
    first_a = jnp.stack([section_layer(section, 0, held_a[section], *shared) for section in range(N_PIPE)])
    first_b = jnp.stack([section_layer(section, 1, held_b[section], *shared) for section in range(N_PIPE)])
    into_a = jnp.concatenate([first_a[1:], new_a[None]], axis=0)
    into_b = jnp.concatenate([new_b[None], first_b[:-1]], axis=0)
    second_a = jnp.stack([section_layer(section, 2, into_a[section], *shared) for section in range(N_PIPE)])
    second_b = jnp.stack([section_layer(section, 3, into_b[section], *shared) for section in range(N_PIPE)])
    return first_a, first_b, second_a, second_b
```

```python
import functools

import jax
import jax.numpy as jnp
import numpy as np
from jax import lax
from jax.experimental import pallas as pl
from jax.experimental.pallas import tpu as pltpu
from jax.sharding import PartitionSpec as P

EXPERTS = 8
TOPK = 2
CAP = 10
D = 7168
TOK = 32
HD = 256
NX, NY, NZ = 2, 4, 4
ROWS = NX * NY * NZ * CAP
BLK = ROWS // 4
PADY = 32
NCH = 7
CW = D // NCH
C1 = 640
C3 = CW - C1
HA = 48
RING = 3
SLOTS_PHASE = 4 * NCH
UNITS = 2 * SLOTS_PHASE
MESH = pl.DeviceIdType.MESH
F32, BF16 = jnp.float32, jnp.bfloat16

X1, Y1, Z3A, Z3B, Z1A, Z1F, X3, Y3 = 0, 1, 4, 6, 8, 10, 12, 13
R1A, Y3R, R1B, X3R, Y1R, R3A, X1R, R3B, PIPE = 16, 18, 21, 23, 24, 27, 29, 30, 32
KINDS = 34


def constants():
    c = np.arange(CAP)
    order1 = np.array(
        [(x, y, z, k) for z in range(NZ) for y in range(NY) for x in range(NX) for k in c]
    )
    order3 = np.array(
        [(x, y, z, k) for y in range(NY) for x in range(NX) for z in range(NZ) for k in c]
    )
    row = lambda o: ((o[:, 0] * NY + o[:, 1]) * NZ + o[:, 2]) * CAP + o[:, 3]
    row1, row3 = row(order1), row(order3)
    from3 = (row1[:, None] == row3[None, :]).astype(np.float32)
    from_saved = (row1[:, None] == np.arange(ROWS)[None, :]).astype(np.float32)
    want3 = (order3[:, 0] * NZ + order3[:, 2]) * 128 + order3[:, 1] * CAP + order3[:, 3]
    want1 = np.full((NY * PADY,), -(1 << 20))
    pick = np.zeros((BLK, NY * PADY), np.float32)
    for y in range(NY):
        for x in range(NX):
            for k in c:
                want1[y * PADY + x * CAP + k] = x * 128 + y * CAP + k
                pick[(y * NX + x) * CAP + k, y * PADY + x * CAP + k] = 1
    lane = np.zeros((1, 128), np.float32)
    lane[0] = np.arange(128) // TOK
    off3 = (np.arange(NX * NZ * TOK) // TOK) * 128
    f = lambda a: np.asarray(a, np.float32)
    b = lambda a: np.asarray(a, np.float32).astype(jnp.bfloat16)
    return (
        b(from3),
        b(from3.T),
        b(from_saved),
        b(pick),
        b(pick.T),
        f(want3)[:, None],
        f(want3)[None, :],
        f(want1)[:, None],
        f(want1)[None, :],
        f(off3)[:, None],
        f(off3)[None, :],
        lane,
    )


def dot(a, b):
    return lax.dot_general(a, b, (((1,), (0,)), ((), ())), preferred_element_type=F32)


def dot_t(a, b):
    return lax.dot_general(a, b, (((1,), (1,)), ((), ())), preferred_element_type=F32)


def kernel(
    xa_ref, xb_ref, na_ref, nb_ref, meta_ref, saved_ref, wg_ref, wu_ref, wdn_ref,
    from3_ref, to3_ref, froms_ref, pick_ref, spread_ref,
    w3c_ref, w3r_ref, w1c_ref, w1r_ref, o3c_ref, o3r_ref, lane_ref,
    out_ref,
    xin, wgu, wd, svd, mr, a1, a1t, pr1, a3, a3t, pr3, fg, fu, acc1, acc3, gu1, gu3,
    t1, y1, z1, t3, y3, y1s, y3s,
    q1, s1, r1a, r1b, y1rs, y1rr, tb1, x1r, q3, y3r, tb3, x3r, v3, s3, r3a, r3b,
    ss, rs, mss, mrs, ls,
):
    me = lax.axis_index("expert")
    pp = lax.axis_index("pipe")
    x, y, z = me // (NY * NZ), (me // NZ) % NY, me % NZ
    core = pp % 2
    xn = 1 - x
    za = (z + 1 + 2 * core) % NZ
    zb = (z + 3 - 2 * core) % NZ
    z2 = (z + 2) % NZ

    def dev(px, py, pz):
        return {"expert": (px * NY + py) * NZ + pz}

    def rcopy(src, dst, kind, g, c, to):
        return pltpu.make_async_remote_copy(
            src_ref=src, dst_ref=dst, send_sem=ss.at[g % RING, kind], recv_sem=rs.at[c, kind],
            device_id=to, device_id_type=MESH,
        )

    def finish(src, landing, kind, g, c, to):
        d = rcopy(src, landing, kind, g, c, to)
        d.wait_send()
        d.wait_recv()

    def load(src, dst, k):
        return pltpu.make_async_copy(src, dst, ls.at[k])

    load(xa_ref, xin.at[0], 0).start()
    load(xb_ref, xin.at[1], 1).start()

    @pl.when(pp == 3)
    def _():
        load(na_ref, xin.at[2], 2).start()

    @pl.when(pp == 0)
    def _():
        load(nb_ref, xin.at[3], 3).start()

    load(saved_ref, svd, 4).start()
    load(wdn_ref, wd, 5).start()
    load(wg_ref, wgu.at[:, 0:HD], 6).start()
    load(wu_ref, wgu.at[:, HD:2 * HD], 7).start()

    barrier = pltpu.get_barrier_semaphore()
    metas = [(dx, dz) for dx in range(NX) for dz in range(NZ) if dx or dz]
    for dx, dz in metas:
        pl.semaphore_signal(barrier, 1, device_id=dev((x + dx) % NX, y, (z + dz) % NZ), device_id_type=MESH)
    for dy in range(1, NY):
        pl.semaphore_signal(barrier, 1, device_id=dev(x, (y + dy) % NY, z), device_id_type=MESH)

    @pl.when(pp > 0)
    def _():
        pl.semaphore_signal(barrier, 1, device_id={"pipe": pp - 1}, device_id_type=MESH)

    @pl.when(pp < 3)
    def _():
        pl.semaphore_signal(barrier, 1, device_id={"pipe": pp + 1}, device_id_type=MESH)

    in_pipe = jnp.where((pp == 0) | (pp == 3), 1, 2)
    pl.semaphore_wait(barrier, len(metas) + NY - 1 + in_pipe)

    src_me = x * NZ + z
    mr[src_me] = meta_ref[...]

    def meta_copy(k, dx, dz, landing):
        return pltpu.make_async_remote_copy(
            src_ref=meta_ref, dst_ref=mr.at[landing], send_sem=mss.at[k], recv_sem=mrs.at[k],
            device_id=dev((x + dx) % NX, y, (z + dz) % NZ), device_id_type=MESH,
        )

    for k, (dx, dz) in enumerate(metas):
        meta_copy(k, dx, dz, src_me).start()

    load(xa_ref, xin.at[0], 0).wait()
    load(xb_ref, xin.at[1], 1).wait()

    @pl.when(pp == 3)
    def _():
        load(na_ref, xin.at[2], 2).wait()

    @pl.when(pp == 0)
    def _():
        load(nb_ref, xin.at[3], 3).wait()

    def col(c, off, width):
        return pl.ds(pl.multiple_of(c * CW + off, 128), width)

    def routes(st, m):
        lane = lane_ref[...]

        def rowpart(s):
            return mr[s, pl.ds(pl.multiple_of(m * 8, 8), 8), :]

        def colpart(s):
            return mr[s, 32:64, :]

        def lanes(parts):
            r = parts[-1]
            for i in range(len(parts) - 2, -1, -1):
                r = jnp.where(lane == float(i), parts[i], r)
            return r

        lane_no = lax.broadcasted_iota(jnp.int32, (1, 128), 1)

        def column(arr, k):
            return jnp.sum(jnp.where(lane_no == m * 4 + k, arr, 0.0), axis=1, keepdims=True)

        mine = (x * 40).astype(F32)
        r1 = lanes([rowpart(z), rowpart(NZ + z)])[:, :NX * TOK]
        o1 = o3r_ref[:, :NX * TOK]
        w1 = w1c_ref[...] + mine
        h0, h1 = w1 == r1[0:1] + o1, w1 == r1[1:2] + o1
        a1[st] = jnp.where(h0 | h1, 1.0, 0.0).astype(BF16)
        pr1[st] = jnp.sum(jnp.where(h0, r1[2:3], 0.0) + jnp.where(h1, r1[3:4], 0.0), axis=1, keepdims=True)
        c1 = jnp.concatenate([colpart(z), colpart(NZ + z)], axis=0)
        o1c = o3c_ref[:NX * TOK, :]
        w1t = w1r_ref[...] + mine
        a1t[st] = jnp.where(
            (column(c1, 0) + o1c == w1t) | (column(c1, 1) + o1c == w1t), 1.0, 0.0
        ).astype(BF16)
        r3 = jnp.concatenate([lanes([rowpart(s) for s in range(4)]), lanes([rowpart(s) for s in range(4, 8)])], axis=1)
        o3 = o3r_ref[...]
        w3 = w3c_ref[...] + mine
        h0, h1 = w3 == r3[0:1] + o3, w3 == r3[1:2] + o3
        a3[st] = jnp.where(h0 | h1, 1.0, 0.0).astype(BF16)
        pr3[st] = jnp.sum(jnp.where(h0, r3[2:3], 0.0) + jnp.where(h1, r3[3:4], 0.0), axis=1, keepdims=True)
        c3 = mr[:, 32:64, :].reshape(NX * NZ * TOK, 128)
        o3t = o3c_ref[...]
        w3t = w3r_ref[...] + mine
        a3t[st] = jnp.where(
            (column(c3, 0) + o3t == w3t) | (column(c3, 1) + o3t == w3t), 1.0, 0.0
        ).astype(BF16)

    def factors(st, m):
        gu = dot(froms_ref[...], svd[m])
        gate, up = gu[:, :HD], gu[:, HD:]
        sig = jax.nn.sigmoid(gate)
        fg[st] = up * sig * (1.0 + gate * (1.0 - sig))
        fu[st] = gate * sig

    def to_y(src_of, buf, st, c, g, kind):
        for dy in range(1, NY):
            yd = (y + dy) % NY
            rcopy(src_of(yd), buf.at[st, c, y], kind + dy - 1, g, c, dev(x, yd, z)).start()

    def from_y(src_of, buf, st, c, g, kind):
        for dy in range(1, NY):
            yd, ys = (y + dy) % NY, (y - dy + NY) % NY
            finish(src_of(yd), buf.at[st, c, ys], kind + dy - 1, g, c, dev(x, yd, z))

    def d0(p, st, c, g):
        m = 2 * p + st

        @pl.when((p == 1) & (((st == 0) & (pp < 3)) | ((st == 1) & (pp > 0))))
        def _():
            landing = xin.at[m, :, col(c, 0, CW)]
            rcopy(landing, landing, PIPE + st, g, c, {"pipe": pp}).wait_recv()

        t1[st, c, x] = xin[m, :, col(c, 0, C1)]
        rcopy(t1.at[st, c, x], t1.at[st, c, x], X1, g, c, dev(xn, y, z)).start()
        t3[st, c, x, z] = xin[m, :, col(c, C1, C3)]
        mine = t3.at[st, c, x, z]
        rcopy(mine, mine, Z3A, g, c, dev(x, y, za)).start()
        rcopy(mine, mine, Z3A + 1, g, c, dev(x, y, zb)).start()

        @pl.when(c == 0)
        def _():
            @pl.when(g == 0)
            def _():
                for k, (dx, dz) in enumerate(metas):
                    landing = ((x + dx) % NX) * NZ + (z - dz + NZ) % NZ
                    d = meta_copy(k, dx, dz, landing)
                    d.wait_send()
                    d.wait_recv()

            routes(st, m)

    def d1(p, st, c, g):
        finish(t1.at[st, c, x], t1.at[st, c, xn], X1, g, c, dev(xn, y, z))
        rows = dot(a1[st], t1[st, c].reshape(NX * TOK, C1)) * pr1[st]
        ring = g % RING
        y1s[ring] = rows.astype(BF16).reshape(NY, PADY, C1)
        to_y(lambda yd: y1s.at[ring, yd], y1, st, c, g, Y1)
        y1[st, c, y] = y1s[ring, y]
        mine = t3.at[st, c, x, z]
        finish(mine, t3.at[st, c, x, zb], Z3A, g, c, dev(x, y, za))
        finish(mine, t3.at[st, c, x, za], Z3A + 1, g, c, dev(x, y, zb))
        fwd_a, fwd_b = t3.at[st, c, x, zb, 0:16], t3.at[st, c, x, za, 16:32]
        rcopy(fwd_a, fwd_a, Z3B, g, c, dev(x, y, za)).start()
        rcopy(fwd_b, fwd_b, Z3B + 1, g, c, dev(x, y, zb)).start()

    def d2(p, st, c, g):
        ring = g % RING
        from_y(lambda yd: y1s.at[ring, yd], y1, st, c, g, Y1)
        z1[st, c, z] = dot(pick_ref[...], y1[st, c].reshape(NY * PADY, C1)).astype(BF16)
        mine = z1.at[st, c, z]
        rcopy(mine, mine, Z1A, g, c, dev(x, y, za)).start()
        rcopy(mine, mine, Z1A + 1, g, c, dev(x, y, zb)).start()
        finish(t3.at[st, c, x, zb, 0:16], t3.at[st, c, x, z2, 0:16], Z3B, g, c, dev(x, y, za))
        finish(t3.at[st, c, x, za, 16:32], t3.at[st, c, x, z2, 16:32], Z3B + 1, g, c, dev(x, y, zb))
        rcopy(t3.at[st, c, x], t3.at[st, c, x], X3, g, c, dev(xn, y, z)).start()

        @pl.when(c == 0)
        def _():
            @pl.when(g == 0)
            def _():
                load(saved_ref, svd, 4).wait()

            factors(st, 2 * p + st)

    def d3(p, st, c, g):
        ring = g % RING
        mine = z1.at[st, c, z]
        finish(mine, z1.at[st, c, zb], Z1A, g, c, dev(x, y, za))
        finish(mine, z1.at[st, c, za], Z1A + 1, g, c, dev(x, y, zb))
        fwd_a, fwd_b = z1.at[st, c, zb, 0:HA], z1.at[st, c, za, HA:BLK]
        rcopy(fwd_a, fwd_a, Z1F, g, c, dev(x, y, za)).start()
        rcopy(fwd_b, fwd_b, Z1F + 1, g, c, dev(x, y, zb)).start()
        finish(t3.at[st, c, x], t3.at[st, c, xn], X3, g, c, dev(xn, y, z))
        rows = dot(a3[st], t3[st, c].reshape(NX * NZ * TOK, C3)) * pr3[st]
        y3s[ring] = rows.astype(BF16).reshape(NY, BLK, C3)
        to_y(lambda yd: y3s.at[ring, yd], y3, st, c, g, Y3)
        y3[st, c, y] = y3s[ring, y]

    def d4(p, st, c, g):
        ring = g % RING
        finish(z1.at[st, c, zb, 0:HA], z1.at[st, c, z2, 0:HA], Z1F, g, c, dev(x, y, za))
        finish(z1.at[st, c, za, HA:BLK], z1.at[st, c, z2, HA:BLK], Z1F + 1, g, c, dev(x, y, zb))
        from_y(lambda yd: y3s.at[ring, yd], y3, st, c, g, Y3)

        @pl.when(g == 0)
        def _():
            load(wdn_ref, wd, 5).wait()

        h1 = dot_t(z1[st, c].reshape(ROWS, C1), wd[:, col(c, 0, C1)])
        h3 = dot_t(y3[st, c].reshape(ROWS, C3), wd[:, col(c, C1, C3)])

        @pl.when(c == 0)
        def _():
            acc1[st] = h1
            acc3[st] = h3

        @pl.when(c > 0)
        def _():
            acc1[st] += h1
            acc3[st] += h3

        @pl.when(c == NCH - 1)
        def _():
            other = acc3[st]
            high = other.astype(BF16)
            low = (other - high.astype(F32)).astype(BF16)
            h = acc1[st] + dot(from3_ref[...], high) + dot(from3_ref[...], low)
            gu1[st, :, 0:HD] = (h * fg[st]).astype(BF16)
            gu1[st, :, HD:2 * HD] = (h * fu[st]).astype(BF16)
            gu3[st] = dot(to3_ref[...], gu1[st]).astype(BF16)

    def r0(p, st, c, g):
        ring = g % RING

        @pl.when(g == 2 * NCH)
        def _():
            load(wg_ref, wgu.at[:, 0:HD], 6).wait()
            load(wu_ref, wgu.at[:, HD:2 * HD], 7).wait()

        part1 = dot_t(gu1[st], wgu[pl.ds(pl.multiple_of(c * CW, 128), C1), :])
        q1[ring] = part1.astype(BF16).reshape(NZ, BLK, C1)
        rcopy(q1.at[ring, z2, 0:HA], r1a.at[st, c, 0:HA], R1A, g, c, dev(x, y, za)).start()
        rcopy(q1.at[ring, z2, HA:BLK], r1a.at[st, c, HA:BLK], R1A + 1, g, c, dev(x, y, zb)).start()
        part3 = dot_t(gu3[st], wgu[pl.ds(pl.multiple_of(c * CW + C1, 128), C3), :])
        q3[ring] = part3.astype(BF16).reshape(NY, BLK, C3)
        to_y(lambda yd: q3.at[ring, yd], y3r, st, c, g, Y3R)
        y3r[st, c, y] = q3[ring, y]

    def r1(p, st, c, g):
        ring = g % RING
        finish(q1.at[ring, z2, 0:HA], r1a.at[st, c, 0:HA], R1A, g, c, dev(x, y, za))
        finish(q1.at[ring, z2, HA:BLK], r1a.at[st, c, HA:BLK], R1A + 1, g, c, dev(x, y, zb))
        s1[ring, 0, 0:HA] = (q1[ring, za, 0:HA].astype(F32) + r1a[st, c, 0:HA].astype(F32)).astype(BF16)
        s1[ring, 0, HA:BLK] = q1[ring, za, HA:BLK]
        rcopy(s1.at[ring, 0], r1b.at[st, c, 0], R1B, g, c, dev(x, y, za)).start()
        s1[ring, 1, 0:HA] = q1[ring, zb, 0:HA]
        s1[ring, 1, HA:BLK] = (q1[ring, zb, HA:BLK].astype(F32) + r1a[st, c, HA:BLK].astype(F32)).astype(BF16)
        rcopy(s1.at[ring, 1], r1b.at[st, c, 1], R1B + 1, g, c, dev(x, y, zb)).start()
        from_y(lambda yd: q3.at[ring, yd], y3r, st, c, g, Y3R)
        sums = dot(a3t[st], y3r[st, c].reshape(ROWS, C3))
        tb3[ring] = sums.astype(BF16).reshape(NX, NZ * TOK, C3)
        rcopy(tb3.at[ring, xn], x3r.at[st, c], X3R, g, c, dev(xn, y, z)).start()

    def r2(p, st, c, g):
        ring = g % RING
        finish(s1.at[ring, 0], r1b.at[st, c, 0], R1B, g, c, dev(x, y, za))
        finish(s1.at[ring, 1], r1b.at[st, c, 1], R1B + 1, g, c, dev(x, y, zb))
        total = q1[ring, z].astype(F32) + r1b[st, c, 0].astype(F32) + r1b[st, c, 1].astype(F32)
        rows = dot(spread_ref[...], total.astype(BF16))
        y1rs[ring] = rows.astype(BF16).reshape(NY, PADY, C1)
        to_y(lambda yd: y1rs.at[ring, yd], y1rr, st, c, g, Y1R)
        y1rr[st, c, y] = y1rs[ring, y]
        finish(tb3.at[ring, xn], x3r.at[st, c], X3R, g, c, dev(xn, y, z))
        v = tb3[ring, x].astype(F32) + x3r[st, c].astype(F32)
        v3[ring] = v.astype(BF16).reshape(NZ, TOK, C3)
        rcopy(v3.at[ring, z2, 0:16], r3a.at[st, c, 0:16], R3A, g, c, dev(x, y, za)).start()
        rcopy(v3.at[ring, z2, 16:32], r3a.at[st, c, 16:32], R3A + 1, g, c, dev(x, y, zb)).start()

    def r3(p, st, c, g):
        ring = g % RING
        from_y(lambda yd: y1rs.at[ring, yd], y1rr, st, c, g, Y1R)
        sums = dot(a1t[st], y1rr[st, c].reshape(NY * PADY, C1))
        tb1[ring] = sums.astype(BF16).reshape(NX, TOK, C1)
        rcopy(tb1.at[ring, xn], x1r.at[st, c], X1R, g, c, dev(xn, y, z)).start()
        finish(v3.at[ring, z2, 0:16], r3a.at[st, c, 0:16], R3A, g, c, dev(x, y, za))
        finish(v3.at[ring, z2, 16:32], r3a.at[st, c, 16:32], R3A + 1, g, c, dev(x, y, zb))
        s3[ring, 0, 0:16] = (v3[ring, za, 0:16].astype(F32) + r3a[st, c, 0:16].astype(F32)).astype(BF16)
        s3[ring, 0, 16:32] = v3[ring, za, 16:32]
        rcopy(s3.at[ring, 0], r3b.at[st, c, 0], R3B, g, c, dev(x, y, za)).start()
        s3[ring, 1, 0:16] = v3[ring, zb, 0:16]
        s3[ring, 1, 16:32] = (v3[ring, zb, 16:32].astype(F32) + r3a[st, c, 16:32].astype(F32)).astype(BF16)
        rcopy(s3.at[ring, 1], r3b.at[st, c, 1], R3B + 1, g, c, dev(x, y, zb)).start()

    def pipe_copy(m, st, c, g, to):
        cols = col(c, 0, CW)
        return rcopy(out_ref.at[m, :, cols], xin.at[m + 2, :, cols], PIPE + st, g, c, {"pipe": to})

    def r4(p, st, c, g):
        ring = g % RING
        m = 2 * p + st
        finish(tb1.at[ring, xn], x1r.at[st, c], X1R, g, c, dev(xn, y, z))
        finish(s3.at[ring, 0], r3b.at[st, c, 0], R3B, g, c, dev(x, y, za))
        finish(s3.at[ring, 1], r3b.at[st, c, 1], R3B + 1, g, c, dev(x, y, zb))
        cols1, cols3 = col(c, 0, C1), col(c, C1, C3)
        o1 = xin[m, :, cols1].astype(F32) + (tb1[ring, x].astype(F32) + x1r[st, c].astype(F32))
        out_ref[m, :, cols1] = o1.astype(BF16)
        o3 = xin[m, :, cols3].astype(F32) + (
            v3[ring, z].astype(F32) + r3b[st, c, 0].astype(F32) + r3b[st, c, 1].astype(F32)
        )
        out_ref[m, :, cols3] = o3.astype(BF16)

        @pl.when((p == 0) & (st == 0) & (pp > 0))
        def _():
            pipe_copy(0, 0, c, g, pp - 1).start()

        @pl.when((p == 0) & (st == 1) & (pp < 3))
        def _():
            pipe_copy(1, 1, c, g, pp + 1).start()

    def r5(p, st, c, g):
        @pl.when((p == 0) & (st == 0) & (pp > 0))
        def _():
            pipe_copy(0, 0, c, g, pp - 1).wait_send()

        @pl.when((p == 0) & (st == 1) & (pp < 3))
        def _():
            pipe_copy(1, 1, c, g, pp + 1).wait_send()

    def stage(t, k, returning, body):
        g = jnp.maximum(t - k, 0)
        p, w = g // SLOTS_PHASE, g % SLOTS_PHASE
        inside = (t - k >= 0) & (t - k < UNITS)
        here = (w >= 2 * NCH) if returning else (w < 2 * NCH)

        @pl.when(inside & here)
        def _():
            body(p, (w // NCH) % 2, w % NCH, g)

    def tick(t, carry):
        for k, body in enumerate([d0, d1, d2, d3, d4]):
            stage(t, k, False, body)
        for k, body in enumerate([r0, r1, r2, r3, r4, r5]):
            stage(t, k, True, body)
        return carry

    lax.fori_loop(0, UNITS + 5, tick, 0)


def layers(xa, xb, na, nb, meta, saved, wg, wu, wdn):
    consts = [jnp.asarray(a) for a in constants()]
    any_spec = pl.BlockSpec(memory_space=pl.ANY)
    vmem = pl.BlockSpec(memory_space=pltpu.VMEM)
    V = pltpu.VMEM
    scratch = [
        V((4, TOK, D), BF16),
        V((D, 2 * HD), BF16),
        V((HD, D), BF16),
        V((4, ROWS, 2 * HD), BF16),
        V((NX * NZ, 64, 128), F32),
        V((2, NY * PADY, NX * TOK), BF16),
        V((2, NX * TOK, NY * PADY), BF16),
        V((2, NY * PADY, 1), F32),
        V((2, ROWS, NX * NZ * TOK), BF16),
        V((2, NX * NZ * TOK, ROWS), BF16),
        V((2, ROWS, 1), F32),
        V((2, ROWS, HD), F32),
        V((2, ROWS, HD), F32),
        V((2, ROWS, HD), F32),
        V((2, ROWS, HD), F32),
        V((2, ROWS, 2 * HD), BF16),
        V((2, ROWS, 2 * HD), BF16),
        V((2, NCH, NX, TOK, C1), BF16),
        V((2, NCH, NY, PADY, C1), BF16),
        V((2, NCH, NZ, BLK, C1), BF16),
        V((2, NCH, NX, NZ, TOK, C3), BF16),
        V((2, NCH, NY, BLK, C3), BF16),
        V((RING, NY, PADY, C1), BF16),
        V((RING, NY, BLK, C3), BF16),
        V((RING, NZ, BLK, C1), BF16),
        V((RING, 2, BLK, C1), BF16),
        V((2, NCH, BLK, C1), BF16),
        V((2, NCH, 2, BLK, C1), BF16),
        V((RING, NY, PADY, C1), BF16),
        V((2, NCH, NY, PADY, C1), BF16),
        V((RING, NX, TOK, C1), BF16),
        V((2, NCH, TOK, C1), BF16),
        V((RING, NY, BLK, C3), BF16),
        V((2, NCH, NY, BLK, C3), BF16),
        V((RING, NX, NZ * TOK, C3), BF16),
        V((2, NCH, NZ * TOK, C3), BF16),
        V((RING, NZ, TOK, C3), BF16),
        V((RING, 2, TOK, C3), BF16),
        V((2, NCH, TOK, C3), BF16),
        V((2, NCH, 2, TOK, C3), BF16),
        pltpu.SemaphoreType.DMA((RING, KINDS)),
        pltpu.SemaphoreType.DMA((NCH, KINDS)),
        pltpu.SemaphoreType.DMA((8,)),
        pltpu.SemaphoreType.DMA((8,)),
        pltpu.SemaphoreType.DMA((8,)),
    ]
    flops = 4 * 2 * ROWS * D * HD * 3
    return pl.pallas_call(
        kernel,
        out_shape=jax.ShapeDtypeStruct((4, TOK, D), BF16),
        in_specs=[any_spec] * 4 + [vmem] + [any_spec] * 4 + [vmem] * len(consts),
        out_specs=vmem,
        scratch_shapes=scratch,
        compiler_params=pltpu.CompilerParams(
            collective_id=0, has_side_effects=True, vmem_limit_bytes=63 * 2**20
        ),
        cost_estimate=pl.CostEstimate(flops=flops, bytes_accessed=16 * 2**20, transcendentals=0),
        name="relay_layers",
    )(xa, xb, na, nb, meta, saved, wg, wu, wdn, *consts)


def route_data(ids, probs):
    micro = ids.shape[0]
    flat = ids.reshape(micro, TOK * TOPK)
    onehot = (flat[:, :, None] == jnp.arange(EXPERTS, dtype=jnp.int32)).astype(jnp.int32)
    ranking = jnp.sum((jnp.cumsum(onehot, axis=1) - 1) * onehot, axis=2)
    slots = (flat * CAP + ranking).reshape(micro, TOK, TOPK).astype(F32)
    both = jnp.concatenate([slots, probs], axis=2)
    by_row = jnp.tile(both.transpose(0, 2, 1), (1, 1, 128 // TOK))
    by_row = jnp.pad(by_row, ((0, 0), (0, 4), (0, 0))).reshape(micro * 8, 128)
    by_col = both.transpose(1, 0, 2).reshape(TOK, micro * 4)
    by_col = jnp.pad(by_col, ((0, 0), (0, 128 - micro * 4)))
    return jnp.concatenate([by_row, by_col], axis=0)


def per_device(
    held_a, held_b, new_a, new_b, expert_ids, route_probs, saved_gate_up, w_gate, w_up, w_down
):
    meta = route_data(expert_ids[0], route_probs[0])
    saved = saved_gate_up[0].reshape(4, ROWS, 2 * HD)
    out = layers(
        held_a[0], held_b[0], new_a, new_b, meta, saved, w_gate[0], w_up[0], w_down[0]
    )
    return out[0][None], out[1][None], out[2][None], out[3][None]


def solution(mesh):
    in_specs = (
        P("pipe", "expert", None),
        P("pipe", "expert", None),
        P("expert", None),
        P("expert", None),
        P("pipe", None, "expert", None),
        P("pipe", None, "expert", None),
        P("pipe", None, None, None, "expert"),
        P("pipe", None, "expert"),
        P("pipe", None, "expert"),
        P("pipe", "expert", None),
    )
    out_specs = (P("pipe", "expert", None),) * 4
    return jax.shard_map(
        per_device, mesh=mesh, in_specs=in_specs, out_specs=out_specs, check_vma=False
    )
```

```python
import functools

import jax
import jax.numpy as jnp
import numpy as np
from jax import lax
from jax.experimental import pallas as pl
from jax.experimental.pallas import tpu as pltpu
from jax.sharding import PartitionSpec as P

EXPERTS = 8
TOPK = 2
CAP = 10
D = 7168
TOK = 32
HD = 256
NX, NY, NZ = 2, 4, 4
ROWS = NX * NY * NZ * CAP
BLK = ROWS // 4
RUN = NX * CAP
NCH = 7
CW = D // NCH
C1 = 640
C3 = CW - C1
KG = C1 // 128
PADY = -(-KG * RUN // 16) * 16
HA = 48
GAP = 2
RING = GAP + 1
DEEP = 2 * GAP + 1
SLOTS_PHASE = 4 * NCH
UNITS = 2 * SLOTS_PHASE
MESH = pl.DeviceIdType.MESH
F32, BF16 = jnp.float32, jnp.bfloat16

X1, Y1, Z3A, Z3B, Z1A, Z1F, X3, Y3 = 0, 1, 4, 6, 8, 10, 12, 13
R1A, Y3R, R1B, X3R, Y1R, R3A, X1R, R3B, PIPE = 16, 18, 21, 23, 24, 27, 29, 30, 32
KINDS = 34


def constants():
    c = np.arange(CAP)
    order1 = np.array(
        [(x, y, z, k) for z in range(NZ) for y in range(NY) for x in range(NX) for k in c]
    )
    order3 = np.array(
        [(x, y, z, k) for y in range(NY) for x in range(NX) for z in range(NZ) for k in c]
    )
    row = lambda o: ((o[:, 0] * NY + o[:, 1]) * NZ + o[:, 2]) * CAP + o[:, 3]
    row1, row3 = row(order1), row(order3)
    from3 = (row1[:, None] == row3[None, :]).astype(np.float32)
    from_saved = np.concatenate(
        [(2 * row1 + i)[:, None] == np.arange(2 * ROWS)[None, :] for i in range(2)], axis=0
    )
    want3 = (order3[:, 0] * NZ + order3[:, 2]) * 128 + order3[:, 1] * CAP + order3[:, 3]
    want1 = np.full((NY * PADY,), -(1 << 20))
    pick = np.zeros((KG * BLK, NY * PADY), np.float32)
    for y in range(NY):
        for group in range(KG):
            for r in range(RUN):
                i = y * PADY + group * RUN + r
                want1[i] = group * 1024 + (r // CAP) * 128 + y * CAP + r % CAP
                pick[group * BLK + y * RUN + r, i] = 1
    off1 = np.array([k * 1024 + x * 128 for x in range(NX) for k in range(KG) for t in range(TOK)])
    lane = np.zeros((1, 128), np.float32)
    lane[0] = np.arange(128) // TOK
    off3 = (np.arange(NX * NZ * TOK) // TOK) * 128
    f = lambda a: np.asarray(a, np.float32)
    b = lambda a: np.asarray(a, np.float32).astype(jnp.bfloat16)
    return (
        b(from3),
        b(from3.T),
        b(from_saved),
        b(pick),
        b(pick.T),
        f(want3)[:, None],
        f(want3)[None, :],
        f(want1)[:, None],
        f(want1)[None, :],
        f(off3)[:, None],
        f(off3)[None, :],
        f(off1)[:, None],
        f(off1)[None, :],
        lane,
    )


def dot(a, b):
    return lax.dot_general(a, b, (((1,), (0,)), ((), ())), preferred_element_type=F32)


def dot_t(a, b):
    return lax.dot_general(a, b, (((1,), (1,)), ((), ())), preferred_element_type=F32)


def kernel(
    xa_ref, xb_ref, na_ref, nb_ref, meta_ref, saved_ref, wg_ref, wu_ref, wdn_ref,
    from3_ref, to3_ref, froms_ref, pick_ref, spread_ref,
    w3c_ref, w3r_ref, w1c_ref, w1r_ref, o3c_ref, o3r_ref, o1c_ref, o1r_ref, lane_ref,
    out_ref,
    xin, ob, wgu, wd, svd, mr, mt, a1, a1t, pr1, a3, a3t, pr3, fg, fu, acc1, acc3, gu1, gu3,
    t1, y1, z1, t3, y3, y1s, y3s,
    q1, s1, r1a, r1b, y1rs, y1rr, tb1, x1r, q3, y3r, tb3, x3r, v3, s3, r3a, r3b,
    ss, rs, mss, mrs, ls, os,
):
    me = lax.axis_index("expert")
    pp = lax.axis_index("pipe")
    x, y, z = me // (NY * NZ), (me // NZ) % NY, me % NZ
    core = pp % 2
    xn = 1 - x
    za = (z + 1 + 2 * core) % NZ
    zb = (z + 3 - 2 * core) % NZ
    z2 = (z + 2) % NZ

    def dev(px, py, pz):
        return {"expert": (px * NY + py) * NZ + pz}

    def rcopy(src, dst, kind, g, c, to):
        return pltpu.make_async_remote_copy(
            src_ref=src, dst_ref=dst, send_sem=ss.at[g % RING, kind], recv_sem=rs.at[c, kind],
            device_id=to, device_id_type=MESH,
        )

    def finish(src, landing, kind, g, c, to):
        d = rcopy(src, landing, kind, g, c, to)
        d.wait_send()
        d.wait_recv()

    def load(src, dst, k):
        return pltpu.make_async_copy(src, dst, ls.at[k])

    load(xa_ref, xin.at[0], 0).start()
    load(xb_ref, xin.at[1], 1).start()

    @pl.when(pp == 3)
    def _():
        load(na_ref, xin.at[2], 2).start()

    @pl.when(pp == 0)
    def _():
        load(nb_ref, xin.at[3], 3).start()

    load(saved_ref, svd, 4).start()
    load(wdn_ref, wd, 5).start()
    load(wg_ref, wgu.at[:, 0:HD], 6).start()
    load(wu_ref, wgu.at[:, HD:2 * HD], 7).start()

    barrier = pltpu.get_barrier_semaphore()
    metas = [(dx, dz) for dx in range(NX) for dz in range(NZ) if dx or dz]
    for dx, dz in metas:
        pl.semaphore_signal(barrier, 1, device_id=dev((x + dx) % NX, y, (z + dz) % NZ), device_id_type=MESH)
    for dy in range(1, NY):
        pl.semaphore_signal(barrier, 1, device_id=dev(x, (y + dy) % NY, z), device_id_type=MESH)

    @pl.when(pp > 0)
    def _():
        pl.semaphore_signal(barrier, 1, device_id={"pipe": pp - 1}, device_id_type=MESH)

    @pl.when(pp < 3)
    def _():
        pl.semaphore_signal(barrier, 1, device_id={"pipe": pp + 1}, device_id_type=MESH)

    in_pipe = jnp.where((pp == 0) | (pp == 3), 1, 2)
    pl.semaphore_wait(barrier, len(metas) + NY - 1 + in_pipe)

    src_me = x * NZ + z
    mr[src_me] = meta_ref[...]

    def meta_copy(k, dx, dz, landing):
        return pltpu.make_async_remote_copy(
            src_ref=meta_ref, dst_ref=mr.at[landing], send_sem=mss.at[k], recv_sem=mrs.at[k],
            device_id=dev((x + dx) % NX, y, (z + dz) % NZ), device_id_type=MESH,
        )

    for k, (dx, dz) in enumerate(metas):
        meta_copy(k, dx, dz, src_me).start()

    load(xa_ref, xin.at[0], 0).wait()
    load(xb_ref, xin.at[1], 1).wait()

    @pl.when(pp == 3)
    def _():
        load(na_ref, xin.at[2], 2).wait()

    @pl.when(pp == 0)
    def _():
        load(nb_ref, xin.at[3], 3).wait()

    def col(c, off, width):
        return pl.ds(pl.multiple_of(c * CW + off, 128), width)

    def routes(st, m):
        lane = lane_ref[...]

        def rowpart(s):
            return mr[s, pl.ds(pl.multiple_of(m * 8, 8), 8), :]

        def lanes(parts):
            r = parts[-1]
            for i in range(len(parts) - 2, -1, -1):
                r = jnp.where(lane == float(i), parts[i], r)
            return r

        lane_no = lax.broadcasted_iota(jnp.int32, (1, TOK), 1)

        def column(arr, k):
            return jnp.sum(jnp.where(lane_no == m * 8 + k, arr, 0.0), axis=1, keepdims=True)

        mine = (x * 40).astype(F32)
        near, far = rowpart(z), rowpart(NZ + z)
        r1 = jnp.concatenate([near, jnp.where(lane == 0.0, near, far), far], axis=1)[:, :NX * KG * TOK]
        o1 = o1r_ref[...]
        w1 = w1c_ref[...] + mine
        h0, h1 = w1 == r1[0:1] + o1, w1 == r1[1:2] + o1
        a1[st] = jnp.where(h0 | h1, 1.0, 0.0).astype(BF16)
        pr1[st] = jnp.sum(jnp.where(h0, r1[2:3], 0.0) + jnp.where(h1, r1[3:4], 0.0), axis=1, keepdims=True)
        c1 = jnp.concatenate([mt[z]] * KG + [mt[NZ + z]] * KG, axis=0)
        o1c = o1c_ref[...]
        w1t = w1r_ref[...] + mine
        a1t[st] = jnp.where(
            (column(c1, 0) + o1c == w1t) | (column(c1, 1) + o1c == w1t), 1.0, 0.0
        ).astype(BF16)
        r3 = jnp.concatenate([lanes([rowpart(s) for s in range(4)]), lanes([rowpart(s) for s in range(4, 8)])], axis=1)
        o3 = o3r_ref[...]
        w3 = w3c_ref[...] + mine
        h0, h1 = w3 == r3[0:1] + o3, w3 == r3[1:2] + o3
        a3[st] = jnp.where(h0 | h1, 1.0, 0.0).astype(BF16)
        pr3[st] = jnp.sum(jnp.where(h0, r3[2:3], 0.0) + jnp.where(h1, r3[3:4], 0.0), axis=1, keepdims=True)
        c3 = mt[...].reshape(NX * NZ * TOK, TOK)
        o3t = o3c_ref[...]
        w3t = w3r_ref[...] + mine
        a3t[st] = jnp.where(
            (column(c3, 0) + o3t == w3t) | (column(c3, 1) + o3t == w3t), 1.0, 0.0
        ).astype(BF16)

    def factors(st, m):
        gu = dot(froms_ref[...], svd[m])
        gate, up = gu[:ROWS], gu[ROWS:]
        sig = jax.nn.sigmoid(gate)
        fg[st] = up * sig * (1.0 + gate * (1.0 - sig))
        fu[st] = gate * sig

    def to_y(src_of, buf, st, c, g, kind):
        for dy in range(1, NY):
            yd = (y + dy) % NY
            rcopy(src_of(yd), buf.at[st, c, y], kind + dy - 1, g, c, dev(x, yd, z)).start()

    def from_y(src_of, buf, st, c, g, kind):
        for dy in range(1, NY):
            yd, ys = (y + dy) % NY, (y - dy + NY) % NY
            finish(src_of(yd), buf.at[st, c, ys], kind + dy - 1, g, c, dev(x, yd, z))

    def d0(p, st, c, g):
        m = 2 * p + st

        @pl.when((p == 1) & (((st == 0) & (pp < 3)) | ((st == 1) & (pp > 0))))
        def _():
            landing = xin.at[m, :, col(c, 0, CW)]
            rcopy(landing, landing, PIPE + st, g, c, {"pipe": pp}).wait_recv()

        for k in range(KG):
            t1[st, c, x, k] = xin[m, :, col(c, 128 * k, 128)]
        rcopy(t1.at[st, c, x], t1.at[st, c, x], X1, g, c, dev(xn, y, z)).start()
        t3[st, c, x, z] = xin[m, :, col(c, C1, C3)]
        mine = t3.at[st, c, x, z]
        rcopy(mine, mine, Z3A, g, c, dev(x, y, za)).start()
        rcopy(mine, mine, Z3A + 1, g, c, dev(x, y, zb)).start()

        @pl.when(c == 0)
        def _():
            @pl.when(g == 0)
            def _():
                for k, (dx, dz) in enumerate(metas):
                    landing = ((x + dx) % NX) * NZ + (z - dz + NZ) % NZ
                    d = meta_copy(k, dx, dz, landing)
                    d.wait_send()
                    d.wait_recv()
                for i in range(NX * NZ):
                    mt[i] = mr[i].T[:TOK]

            routes(st, m)

    def d1(p, st, c, g):
        finish(t1.at[st, c, x], t1.at[st, c, xn], X1, g, c, dev(xn, y, z))
        rows = dot(a1[st], t1[st, c].reshape(NX * KG * TOK, 128)) * pr1[st]
        ring = g % RING
        y1s[ring] = rows.astype(BF16).reshape(NY, PADY, 128)
        to_y(lambda yd: y1s.at[ring, yd], y1, st, c, g, Y1)
        y1[st, c, y] = y1s[ring, y]
        mine = t3.at[st, c, x, z]
        finish(mine, t3.at[st, c, x, zb], Z3A, g, c, dev(x, y, za))
        finish(mine, t3.at[st, c, x, za], Z3A + 1, g, c, dev(x, y, zb))
        fwd_a, fwd_b = t3.at[st, c, x, zb, 0:16], t3.at[st, c, x, za, 16:32]
        rcopy(fwd_a, fwd_a, Z3B, g, c, dev(x, y, za)).start()
        rcopy(fwd_b, fwd_b, Z3B + 1, g, c, dev(x, y, zb)).start()

    def d2(p, st, c, g):
        ring = g % RING
        from_y(lambda yd: y1s.at[ring, yd], y1, st, c, g, Y1)
        rows = dot(pick_ref[...], y1[st, c].reshape(NY * PADY, 128)).astype(BF16)
        for k in range(KG):
            z1[st, c, z, :, 128 * k:128 * (k + 1)] = rows[k * BLK:(k + 1) * BLK]
        mine = z1.at[st, c, z]
        rcopy(mine, mine, Z1A, g, c, dev(x, y, za)).start()
        rcopy(mine, mine, Z1A + 1, g, c, dev(x, y, zb)).start()
        finish(t3.at[st, c, x, zb, 0:16], t3.at[st, c, x, z2, 0:16], Z3B, g, c, dev(x, y, za))
        finish(t3.at[st, c, x, za, 16:32], t3.at[st, c, x, z2, 16:32], Z3B + 1, g, c, dev(x, y, zb))
        rcopy(t3.at[st, c, x], t3.at[st, c, x], X3, g, c, dev(xn, y, z)).start()

        @pl.when(c == 0)
        def _():
            @pl.when(g == 0)
            def _():
                load(saved_ref, svd, 4).wait()

            factors(st, 2 * p + st)

    def d3(p, st, c, g):
        ring = g % RING
        mine = z1.at[st, c, z]
        finish(mine, z1.at[st, c, zb], Z1A, g, c, dev(x, y, za))
        finish(mine, z1.at[st, c, za], Z1A + 1, g, c, dev(x, y, zb))
        fwd_a, fwd_b = z1.at[st, c, zb, 0:HA], z1.at[st, c, za, HA:BLK]
        rcopy(fwd_a, fwd_a, Z1F, g, c, dev(x, y, za)).start()
        rcopy(fwd_b, fwd_b, Z1F + 1, g, c, dev(x, y, zb)).start()
        finish(t3.at[st, c, x], t3.at[st, c, xn], X3, g, c, dev(xn, y, z))
        rows = dot(a3[st], t3[st, c].reshape(NX * NZ * TOK, C3)) * pr3[st]
        y3s[ring] = rows.astype(BF16).reshape(NY, BLK, C3)
        to_y(lambda yd: y3s.at[ring, yd], y3, st, c, g, Y3)
        y3[st, c, y] = y3s[ring, y]

    def d4(p, st, c, g):
        ring = g % RING
        finish(z1.at[st, c, zb, 0:HA], z1.at[st, c, z2, 0:HA], Z1F, g, c, dev(x, y, za))
        finish(z1.at[st, c, za, HA:BLK], z1.at[st, c, z2, HA:BLK], Z1F + 1, g, c, dev(x, y, zb))
        from_y(lambda yd: y3s.at[ring, yd], y3, st, c, g, Y3)

        @pl.when(g == 0)
        def _():
            load(wdn_ref, wd, 5).wait()

        h1 = dot_t(z1[st, c].reshape(ROWS, C1), wd[:, col(c, 0, C1)])
        h3 = dot_t(y3[st, c].reshape(ROWS, C3), wd[:, col(c, C1, C3)])

        @pl.when(c == 0)
        def _():
            acc1[st] = h1
            acc3[st] = h3

        @pl.when(c > 0)
        def _():
            acc1[st] += h1
            acc3[st] += h3

        @pl.when(c == NCH - 1)
        def _():
            other = acc3[st]
            high = other.astype(BF16)
            low = (other - high.astype(F32)).astype(BF16)
            h = acc1[st] + dot(from3_ref[...], high) + dot(from3_ref[...], low)
            gu1[st, :, 0:HD] = (h * fg[st]).astype(BF16)
            gu1[st, :, HD:2 * HD] = (h * fu[st]).astype(BF16)
            gu3[st] = dot(to3_ref[...], gu1[st]).astype(BF16)

    def r0(p, st, c, g):
        ring, deep = g % RING, g % DEEP

        @pl.when(g == 2 * NCH)
        def _():
            load(wg_ref, wgu.at[:, 0:HD], 6).wait()
            load(wu_ref, wgu.at[:, HD:2 * HD], 7).wait()

        part1 = dot_t(gu1[st], wgu[pl.ds(pl.multiple_of(c * CW, 128), C1), :])
        q1[deep] = part1.astype(BF16).reshape(NZ, BLK, C1)
        rcopy(q1.at[deep, z2, 0:HA], r1a.at[st, c, 0:HA], R1A, g, c, dev(x, y, za)).start()
        rcopy(q1.at[deep, z2, HA:BLK], r1a.at[st, c, HA:BLK], R1A + 1, g, c, dev(x, y, zb)).start()
        part3 = dot_t(gu3[st], wgu[pl.ds(pl.multiple_of(c * CW + C1, 128), C3), :])
        q3[ring] = part3.astype(BF16).reshape(NY, BLK, C3)
        to_y(lambda yd: q3.at[ring, yd], y3r, st, c, g, Y3R)
        y3r[st, c, y] = q3[ring, y]

    def r1(p, st, c, g):
        ring, deep = g % RING, g % DEEP
        finish(q1.at[deep, z2, 0:HA], r1a.at[st, c, 0:HA], R1A, g, c, dev(x, y, za))
        finish(q1.at[deep, z2, HA:BLK], r1a.at[st, c, HA:BLK], R1A + 1, g, c, dev(x, y, zb))
        s1[ring, 0, 0:HA] = (q1[deep, za, 0:HA].astype(F32) + r1a[st, c, 0:HA].astype(F32)).astype(BF16)
        s1[ring, 0, HA:BLK] = q1[deep, za, HA:BLK]
        rcopy(s1.at[ring, 0], r1b.at[st, c, 0], R1B, g, c, dev(x, y, za)).start()
        s1[ring, 1, 0:HA] = q1[deep, zb, 0:HA]
        s1[ring, 1, HA:BLK] = (q1[deep, zb, HA:BLK].astype(F32) + r1a[st, c, HA:BLK].astype(F32)).astype(BF16)
        rcopy(s1.at[ring, 1], r1b.at[st, c, 1], R1B + 1, g, c, dev(x, y, zb)).start()
        from_y(lambda yd: q3.at[ring, yd], y3r, st, c, g, Y3R)
        sums = dot(a3t[st], y3r[st, c].reshape(ROWS, C3))
        tb3[ring] = sums.astype(BF16).reshape(NX, NZ * TOK, C3)
        rcopy(tb3.at[ring, xn], x3r.at[st, c], X3R, g, c, dev(xn, y, z)).start()

    def r2(p, st, c, g):
        ring, deep = g % RING, g % DEEP
        finish(s1.at[ring, 0], r1b.at[st, c, 0], R1B, g, c, dev(x, y, za))
        finish(s1.at[ring, 1], r1b.at[st, c, 1], R1B + 1, g, c, dev(x, y, zb))
        total = q1[deep, z].astype(F32) + r1b[st, c, 0].astype(F32) + r1b[st, c, 1].astype(F32)
        total = total.astype(BF16)
        groups = jnp.concatenate([total[:, 128 * k:128 * (k + 1)] for k in range(KG)], axis=0)
        rows = dot(spread_ref[...], groups)
        y1rs[ring] = rows.astype(BF16).reshape(NY, PADY, 128)
        to_y(lambda yd: y1rs.at[ring, yd], y1rr, st, c, g, Y1R)
        y1rr[st, c, y] = y1rs[ring, y]
        finish(tb3.at[ring, xn], x3r.at[st, c], X3R, g, c, dev(xn, y, z))
        v = tb3[ring, x].astype(F32) + x3r[st, c].astype(F32)
        v3[deep] = v.astype(BF16).reshape(NZ, TOK, C3)
        rcopy(v3.at[deep, z2, 0:16], r3a.at[st, c, 0:16], R3A, g, c, dev(x, y, za)).start()
        rcopy(v3.at[deep, z2, 16:32], r3a.at[st, c, 16:32], R3A + 1, g, c, dev(x, y, zb)).start()

    def r3(p, st, c, g):
        ring, deep = g % RING, g % DEEP
        from_y(lambda yd: y1rs.at[ring, yd], y1rr, st, c, g, Y1R)
        sums = dot(a1t[st], y1rr[st, c].reshape(NY * PADY, 128))
        tb1[ring] = sums.astype(BF16).reshape(NX, KG, TOK, 128)
        rcopy(tb1.at[ring, xn], x1r.at[st, c], X1R, g, c, dev(xn, y, z)).start()
        finish(v3.at[deep, z2, 0:16], r3a.at[st, c, 0:16], R3A, g, c, dev(x, y, za))
        finish(v3.at[deep, z2, 16:32], r3a.at[st, c, 16:32], R3A + 1, g, c, dev(x, y, zb))
        s3[ring, 0, 0:16] = (v3[deep, za, 0:16].astype(F32) + r3a[st, c, 0:16].astype(F32)).astype(BF16)
        s3[ring, 0, 16:32] = v3[deep, za, 16:32]
        rcopy(s3.at[ring, 0], r3b.at[st, c, 0], R3B, g, c, dev(x, y, za)).start()
        s3[ring, 1, 0:16] = v3[deep, zb, 0:16]
        s3[ring, 1, 16:32] = (v3[deep, zb, 16:32].astype(F32) + r3a[st, c, 16:32].astype(F32)).astype(BF16)
        rcopy(s3.at[ring, 1], r3b.at[st, c, 1], R3B + 1, g, c, dev(x, y, zb)).start()

    def out_copy(m, c, ring):
        cols = col(c, 0, CW)
        return pltpu.make_async_copy(ob.at[m, :, cols], out_ref.at[m, :, cols], os.at[ring])

    def pipe_copy(m, st, c, g, to):
        cols = col(c, 0, CW)
        return rcopy(ob.at[m, :, cols], xin.at[m + 2, :, cols], PIPE + st, g, c, {"pipe": to})

    def r4(p, st, c, g):
        ring, deep = g % RING, g % DEEP
        m = 2 * p + st
        finish(tb1.at[ring, xn], x1r.at[st, c], X1R, g, c, dev(xn, y, z))
        finish(s3.at[ring, 0], r3b.at[st, c, 0], R3B, g, c, dev(x, y, za))
        finish(s3.at[ring, 1], r3b.at[st, c, 1], R3B + 1, g, c, dev(x, y, zb))
        for k in range(KG):
            cols = col(c, 128 * k, 128)
            o1 = xin[m, :, cols].astype(F32) + (tb1[ring, x, k].astype(F32) + x1r[st, c, k].astype(F32))
            ob[m, :, cols] = o1.astype(BF16)
        cols3 = col(c, C1, C3)
        o3 = xin[m, :, cols3].astype(F32) + (
            v3[deep, z].astype(F32) + r3b[st, c, 0].astype(F32) + r3b[st, c, 1].astype(F32)
        )
        ob[m, :, cols3] = o3.astype(BF16)
        out_copy(m, c, ring).start()

        @pl.when((p == 0) & (st == 0) & (pp > 0))
        def _():
            pipe_copy(0, 0, c, g, pp - 1).start()

        @pl.when((p == 0) & (st == 1) & (pp < 3))
        def _():
            pipe_copy(1, 1, c, g, pp + 1).start()

    def r5(p, st, c, g):
        out_copy(2 * p + st, c, g % RING).wait()

        @pl.when((p == 0) & (st == 0) & (pp > 0))
        def _():
            pipe_copy(0, 0, c, g, pp - 1).wait_send()

        @pl.when((p == 0) & (st == 1) & (pp < 3))
        def _():
            pipe_copy(1, 1, c, g, pp + 1).wait_send()

    def stage(t, k, returning, body):
        g = jnp.maximum(t - k, 0)
        p, w = g // SLOTS_PHASE, g % SLOTS_PHASE
        inside = (t - k >= 0) & (t - k < UNITS)
        here = (w >= 2 * NCH) if returning else (w < 2 * NCH)

        @pl.when(inside & here)
        def _():
            body(p, (w // NCH) % 2, w % NCH, g)

    def tick(t, carry):
        for k, body in enumerate([d0, d1, d2, d3, d4]):
            stage(t, GAP * k, False, body)
        for k, body in enumerate([r0, r1, r2, r3, r4, r5]):
            stage(t, GAP * k, True, body)
        return carry

    lax.fori_loop(0, UNITS + 5 * GAP, tick, 0)


def layers(xa, xb, na, nb, meta, saved, wg, wu, wdn):
    consts = [jnp.asarray(a) for a in constants()]
    any_spec = pl.BlockSpec(memory_space=pl.ANY)
    vmem = pl.BlockSpec(memory_space=pltpu.VMEM)
    V = pltpu.VMEM
    scratch = [
        V((4, TOK, D), BF16),
        V((4, TOK, D), BF16),
        V((D, 2 * HD), BF16),
        V((HD, D), BF16),
        V((4, 2 * ROWS, HD), BF16),
        V((NX * NZ, 32, 128), F32),
        V((NX * NZ, TOK, TOK), F32),
        V((2, NY * PADY, NX * KG * TOK), BF16),
        V((2, NX * KG * TOK, NY * PADY), BF16),
        V((2, NY * PADY, 1), F32),
        V((2, ROWS, NX * NZ * TOK), BF16),
        V((2, NX * NZ * TOK, ROWS), BF16),
        V((2, ROWS, 1), F32),
        V((2, ROWS, HD), F32),
        V((2, ROWS, HD), F32),
        V((2, ROWS, HD), F32),
        V((2, ROWS, HD), F32),
        V((2, ROWS, 2 * HD), BF16),
        V((2, ROWS, 2 * HD), BF16),
        V((2, NCH, NX, KG, TOK, 128), BF16),
        V((2, NCH, NY, PADY, 128), BF16),
        V((2, NCH, NZ, BLK, C1), BF16),
        V((2, NCH, NX, NZ, TOK, C3), BF16),
        V((2, NCH, NY, BLK, C3), BF16),
        V((RING, NY, PADY, 128), BF16),
        V((RING, NY, BLK, C3), BF16),
        V((DEEP, NZ, BLK, C1), BF16),
        V((RING, 2, BLK, C1), BF16),
        V((2, NCH, BLK, C1), BF16),
        V((2, NCH, 2, BLK, C1), BF16),
        V((RING, NY, PADY, 128), BF16),
        V((2, NCH, NY, PADY, 128), BF16),
        V((RING, NX, KG, TOK, 128), BF16),
        V((2, NCH, KG, TOK, 128), BF16),
        V((RING, NY, BLK, C3), BF16),
        V((2, NCH, NY, BLK, C3), BF16),
        V((RING, NX, NZ * TOK, C3), BF16),
        V((2, NCH, NZ * TOK, C3), BF16),
        V((DEEP, NZ, TOK, C3), BF16),
        V((RING, 2, TOK, C3), BF16),
        V((2, NCH, TOK, C3), BF16),
        V((2, NCH, 2, TOK, C3), BF16),
        pltpu.SemaphoreType.DMA((RING, KINDS)),
        pltpu.SemaphoreType.DMA((NCH, KINDS)),
        pltpu.SemaphoreType.DMA((8,)),
        pltpu.SemaphoreType.DMA((8,)),
        pltpu.SemaphoreType.DMA((8,)),
        pltpu.SemaphoreType.DMA((RING,)),
    ]
    flops = 4 * 2 * ROWS * D * HD * 3
    return pl.pallas_call(
        kernel,
        out_shape=jax.ShapeDtypeStruct((4, TOK, D), BF16),
        in_specs=[any_spec] * 4 + [vmem] + [any_spec] * 4 + [vmem] * len(consts),
        out_specs=any_spec,
        scratch_shapes=scratch,
        compiler_params=pltpu.CompilerParams(
            collective_id=0, has_side_effects=True, vmem_limit_bytes=63 * 2**20
        ),
        cost_estimate=pl.CostEstimate(flops=flops, bytes_accessed=16 * 2**20, transcendentals=0),
        name="relay_layers",
    )(xa, xb, na, nb, meta, saved, wg, wu, wdn, *consts)


def route_data(ids, probs):
    micro = ids.shape[0]
    flat = ids.reshape(micro, TOK * TOPK)
    pair = jnp.arange(TOK * TOPK)
    earlier = (flat[:, :, None] == flat[:, None, :]) & (pair[None, :] < pair[:, None])
    ranking = jnp.sum(earlier.astype(jnp.int32), axis=2)
    slots = (flat * CAP + ranking).reshape(micro, TOK, TOPK).astype(F32)
    both = jnp.concatenate([slots, probs], axis=2)
    by_row = jnp.tile(both.transpose(0, 2, 1), (1, 2, 128 // TOK))
    return by_row.reshape(micro * 8, 128)


def per_device(
    held_a, held_b, new_a, new_b, expert_ids, route_probs, saved_gate_up, w_gate, w_up, w_down
):
    meta = route_data(expert_ids[0], route_probs[0])
    saved = saved_gate_up[0].reshape(4, 2 * ROWS, HD)
    out = layers(
        held_a[0], held_b[0], new_a, new_b, meta, saved, w_gate[0], w_up[0], w_down[0]
    )
    return out[0][None], out[1][None], out[2][None], out[3][None]


def solution(mesh):
    in_specs = (
        P("pipe", "expert", None),
        P("pipe", "expert", None),
        P("expert", None),
        P("expert", None),
        P("pipe", None, "expert", None),
        P("pipe", None, "expert", None),
        P("pipe", None, None, None, "expert"),
        P("pipe", None, "expert"),
        P("pipe", None, "expert"),
        P("pipe", "expert", None),
    )
    out_specs = (P("pipe", "expert", None),) * 4
    return jax.shard_map(
        per_device, mesh=mesh, in_specs=in_specs, out_specs=out_specs, check_vma=False
    )
```

```python
import functools

import jax
import jax.numpy as jnp
import numpy as np
from jax import lax
from jax.experimental import pallas as pl
from jax.experimental.pallas import tpu as pltpu
from jax.sharding import PartitionSpec as P

EXPERTS = 8
TOPK = 2
CAP = 10
D = 7168
TOK = 32
HD = 256
NX, NY, NZ = 2, 4, 4
ROWS = NX * NY * NZ * CAP
BLK = ROWS // 4
RUN = NX * CAP
NCH = 7
CW = D // NCH
C1 = 640
C3 = CW - C1
KG = C1 // 128
PADY = -(-KG * RUN // 16) * 16
HA = 48
S1 = 512
S3 = CW - S1
KD = S1 // 128
PADD = -(-KD * RUN // 16) * 16
H1, H3 = S1 // 2, S3 // 2
GAP = 2
DISPATCH = (0, 2, 4, 6, 8, 10)
RETURN = (2, 4, 6, 8, 10, 12)
RING = GAP + 1
DEEP = 2 * GAP + 1
SLOTS_PHASE = 4 * NCH
UNITS = 2 * SLOTS_PHASE
MESH = pl.DeviceIdType.MESH
F32, BF16 = jnp.float32, jnp.bfloat16

X1, Y1, Z3A, Z3B, Z1A, Z1F, X3, Y3 = 0, 1, 4, 6, 8, 10, 12, 13
R1A, Y3R, R1B, X3R, Y1R, R3A, X1R, R3B, PIPE = 16, 18, 21, 23, 24, 27, 29, 30, 32
KINDS = 34


def constants():
    c = np.arange(CAP)
    order1 = np.array(
        [(x, y, z, k) for z in range(NZ) for y in range(NY) for x in range(NX) for k in c]
    )
    order3 = np.array(
        [(x, y, z, k) for y in range(NY) for x in range(NX) for z in range(NZ) for k in c]
    )
    row = lambda o: ((o[:, 0] * NY + o[:, 1]) * NZ + o[:, 2]) * CAP + o[:, 3]
    row1, row3 = row(order1), row(order3)
    from3 = (row1[:, None] == row3[None, :]).astype(np.float32)
    from_saved = np.concatenate(
        [(2 * row1 + i)[:, None] == np.arange(2 * ROWS)[None, :] for i in range(2)], axis=0
    )
    want3 = (order3[:, 0] * NZ + order3[:, 2]) * 128 + order3[:, 1] * CAP + order3[:, 3]

    def stacked(groups, pad):
        want = np.full((NY * pad,), -(1 << 20))
        pick = np.zeros((groups * BLK, NY * pad), np.float32)
        for y in range(NY):
            for group in range(groups):
                for r in range(RUN):
                    i = y * pad + group * RUN + r
                    want[i] = group * 1024 + (r // CAP) * 128 + y * CAP + r % CAP
                    pick[group * BLK + y * RUN + r, i] = 1
        off = [k * 1024 + x * 128 for x in range(NX) for k in range(groups) for t in range(TOK)]
        return want, pick, np.array(off)

    want1, pick1, off1 = stacked(KD, PADD)
    want1r, pick1r, off1r = stacked(KG, PADY)
    lane = np.zeros((1, 128), np.float32)
    lane[0] = np.arange(128) // TOK
    off3 = (np.arange(NX * NZ * TOK) // TOK) * 128
    f = lambda a: np.asarray(a, np.float32)
    b = lambda a: np.asarray(a, np.float32).astype(jnp.bfloat16)
    return (
        b(from3),
        b(from3.T),
        b(from_saved),
        b(pick1),
        b(pick1r.T),
        f(want3)[:, None],
        f(want3)[None, :],
        f(want1)[:, None],
        f(want1r)[None, :],
        f(off3)[:, None],
        f(off3)[None, :],
        f(off1r)[:, None],
        f(off1)[None, :],
        lane,
    )


def dot(a, b):
    return lax.dot_general(a, b, (((1,), (0,)), ((), ())), preferred_element_type=F32)


def dot_t(a, b):
    return lax.dot_general(a, b, (((1,), (1,)), ((), ())), preferred_element_type=F32)


def kernel(
    xa_ref, xb_ref, na_ref, nb_ref, meta_ref, saved_ref, wg_ref, wu_ref, wdn_ref,
    from3_ref, to3_ref, froms_ref, pick_ref, spread_ref,
    w3c_ref, w3r_ref, w1c_ref, w1r_ref, o3c_ref, o3r_ref, o1c_ref, o1r_ref, lane_ref,
    out_ref,
    xin, ob, wgu, wd, svd, mr, mt, a1, a1t, pr1, a3, a3t, pr3, fg, fu, acc1, acc3, accp, gu1, gu3,
    t1, y1, z1, t3, y3, y1s, y3s, zs, wp, hs, hr,
    q1, s1, r1a, r1b, y1rs, y1rr, tb1, x1r, q3, y3r, tb3, x3r, v3, s3, r3a, r3b,
    ss, rs, mss, mrs, ls, os, wss, wrs, hss, hrs,
):
    me = lax.axis_index("expert")
    pp = lax.axis_index("pipe")
    x, y, z = me // (NY * NZ), (me // NZ) % NY, me % NZ
    core = pp % 2
    xn = 1 - x
    za = (z + 1 + 2 * core) % NZ
    zb = (z + 3 - 2 * core) % NZ
    z2 = (z + 2) % NZ
    near1, near2 = z + 1 - 2 * (z % 2), 3 - z

    def pairing(c):
        q = c % 2
        d = jnp.where(q == 0, near1, near2)
        h = jnp.where(q == 0, near2, near1)
        return q, d, h, jnp.where(q == 0, z // 2, ((z + 1) // 2) % 2)

    def dev(px, py, pz):
        return {"expert": (px * NY + py) * NZ + pz}

    def rcopy(src, dst, kind, g, c, to):
        return pltpu.make_async_remote_copy(
            src_ref=src, dst_ref=dst, send_sem=ss.at[g % RING, kind], recv_sem=rs.at[c, kind],
            device_id=to, device_id_type=MESH,
        )

    def finish(src, landing, kind, g, c, to):
        d = rcopy(src, landing, kind, g, c, to)
        d.wait_send()
        d.wait_recv()

    def load(src, dst, k):
        return pltpu.make_async_copy(src, dst, ls.at[k])

    load(xa_ref, xin.at[0], 0).start()
    load(xb_ref, xin.at[1], 1).start()

    @pl.when(pp == 3)
    def _():
        load(na_ref, xin.at[2], 2).start()

    @pl.when(pp == 0)
    def _():
        load(nb_ref, xin.at[3], 3).start()

    load(saved_ref, svd, 4).start()
    load(wdn_ref, wd, 5).start()
    load(wg_ref, wgu.at[:, 0:HD], 6).start()
    load(wu_ref, wgu.at[:, HD:2 * HD], 7).start()

    barrier = pltpu.get_barrier_semaphore()
    metas = [(dx, dz) for dx in range(NX) for dz in range(NZ) if dx or dz]
    for dx, dz in metas:
        pl.semaphore_signal(barrier, 1, device_id=dev((x + dx) % NX, y, (z + dz) % NZ), device_id_type=MESH)
    for dy in range(1, NY):
        pl.semaphore_signal(barrier, 1, device_id=dev(x, (y + dy) % NY, z), device_id_type=MESH)

    @pl.when(pp > 0)
    def _():
        pl.semaphore_signal(barrier, 1, device_id={"pipe": pp - 1}, device_id_type=MESH)

    @pl.when(pp < 3)
    def _():
        pl.semaphore_signal(barrier, 1, device_id={"pipe": pp + 1}, device_id_type=MESH)

    in_pipe = jnp.where((pp == 0) | (pp == 3), 1, 2)
    pl.semaphore_wait(barrier, len(metas) + NY - 1 + in_pipe)

    src_me = x * NZ + z
    mr[src_me] = meta_ref[...]

    def meta_copy(k, dx, dz, landing):
        return pltpu.make_async_remote_copy(
            src_ref=meta_ref, dst_ref=mr.at[landing], send_sem=mss.at[k], recv_sem=mrs.at[k],
            device_id=dev((x + dx) % NX, y, (z + dz) % NZ), device_id_type=MESH,
        )

    for k, (dx, dz) in enumerate(metas):
        meta_copy(k, dx, dz, src_me).start()

    load(xa_ref, xin.at[0], 0).wait()
    load(xb_ref, xin.at[1], 1).wait()

    @pl.when(pp == 3)
    def _():
        load(na_ref, xin.at[2], 2).wait()

    @pl.when(pp == 0)
    def _():
        load(nb_ref, xin.at[3], 3).wait()

    def col(c, off, width):
        return pl.ds(pl.multiple_of(c * CW + off, 128), width)

    def routes(st, m):
        lane = lane_ref[...]

        def rowpart(s):
            return mr[s, pl.ds(pl.multiple_of(m * 8, 8), 8), :]

        def lanes(parts):
            r = parts[-1]
            for i in range(len(parts) - 2, -1, -1):
                r = jnp.where(lane == float(i), parts[i], r)
            return r

        lane_no = lax.broadcasted_iota(jnp.int32, (1, TOK), 1)

        def column(arr, k):
            return jnp.sum(jnp.where(lane_no == m * 8 + k, arr, 0.0), axis=1, keepdims=True)

        mine = (x * 40).astype(F32)
        near, far = rowpart(z), rowpart(NZ + z)
        r1 = jnp.concatenate([near, far], axis=1)
        o1 = o1r_ref[...]
        w1 = w1c_ref[...] + mine
        h0, h1 = w1 == r1[0:1] + o1, w1 == r1[1:2] + o1
        a1[st] = jnp.where(h0 | h1, 1.0, 0.0).astype(BF16)
        pr1[st] = jnp.sum(jnp.where(h0, r1[2:3], 0.0) + jnp.where(h1, r1[3:4], 0.0), axis=1, keepdims=True)
        c1 = jnp.concatenate([mt[z]] * KG + [mt[NZ + z]] * KG, axis=0)
        o1c = o1c_ref[...]
        w1t = w1r_ref[...] + mine
        a1t[st] = jnp.where(
            (column(c1, 0) + o1c == w1t) | (column(c1, 1) + o1c == w1t), 1.0, 0.0
        ).astype(BF16)
        r3 = jnp.concatenate([lanes([rowpart(s) for s in range(4)]), lanes([rowpart(s) for s in range(4, 8)])], axis=1)
        o3 = o3r_ref[...]
        w3 = w3c_ref[...] + mine
        h0, h1 = w3 == r3[0:1] + o3, w3 == r3[1:2] + o3
        a3[st] = jnp.where(h0 | h1, 1.0, 0.0).astype(BF16)
        pr3[st] = jnp.sum(jnp.where(h0, r3[2:3], 0.0) + jnp.where(h1, r3[3:4], 0.0), axis=1, keepdims=True)
        c3 = mt[...].reshape(NX * NZ * TOK, TOK)
        o3t = o3c_ref[...]
        w3t = w3r_ref[...] + mine
        a3t[st] = jnp.where(
            (column(c3, 0) + o3t == w3t) | (column(c3, 1) + o3t == w3t), 1.0, 0.0
        ).astype(BF16)

    def factors(st, m):
        gu = dot(froms_ref[...], svd[m])
        gate, up = gu[:ROWS], gu[ROWS:]
        sig = jax.nn.sigmoid(gate)
        fg[st] = up * sig * (1.0 + gate * (1.0 - sig))
        fu[st] = gate * sig

    def to_y(src_of, buf, st, c, g, kind):
        for dy in range(1, NY):
            yd = (y + dy) % NY
            rcopy(src_of(yd), buf.at[st, c, y], kind + dy - 1, g, c, dev(x, yd, z)).start()

    def from_y(src_of, buf, st, c, g, kind):
        for dy in range(1, NY):
            yd, ys = (y + dy) % NY, (y - dy + NY) % NY
            finish(src_of(yd), buf.at[st, c, ys], kind + dy - 1, g, c, dev(x, yd, z))

    def half_col(c, off, half, width):
        return pl.ds(pl.multiple_of(c * CW + off + half * width, 128), width)

    def weights(c, h, half, piece):
        cols = half_col(c, piece * S1, 1 - half, H1)
        return pltpu.make_async_remote_copy(
            src_ref=wd.at[:, cols], dst_ref=wp.at[c, piece], send_sem=wss.at[c, piece],
            recv_sem=wrs.at[c, piece], device_id=dev(x, y, h), device_id_type=MESH,
        )

    def partials(st, q, h):
        return pltpu.make_async_remote_copy(
            src_ref=hs.at[q], dst_ref=hr.at[st, q], send_sem=hss.at[q],
            recv_sem=hrs.at[st, q], device_id=dev(x, y, h), device_id_type=MESH,
        )

    def reorder(a):
        high = a.astype(BF16)
        low = (a - high.astype(F32)).astype(BF16)
        return dot(from3_ref[...], high) + dot(from3_ref[...], low)

    def d0(p, st, c, g):
        m = 2 * p + st

        @pl.when((p == 1) & (((st == 0) & (pp < 3)) | ((st == 1) & (pp > 0))))
        def _():
            landing = xin.at[m, :, col(c, 0, CW)]
            rcopy(landing, landing, PIPE + st, g, c, {"pipe": pp}).wait_recv()

        q, d, h, half = pairing(c)
        for k in range(KD):
            t1[st, c, x, k] = xin[m, :, col(c, 128 * k, 128)]
        rcopy(t1.at[st, c, x], t1.at[st, c, x], X1, g, c, dev(xn, y, z)).start()
        t3[st, c, x, z] = xin[m, :, half_col(c, S1, half, H3)]
        mine = t3.at[st, c, x, z]
        rcopy(mine, mine, Z3A + q, g, c, dev(x, y, d)).start()
        rcopy(xin.at[m, :, half_col(c, S1, 1 - half, H3)], mine, Z3A + 1 - q, g, c, dev(x, y, h)).start()

        @pl.when((p == 0) & (st == 0))
        def _():
            @pl.when(g == 0)
            def _():
                load(wdn_ref, wd, 5).wait()

            weights(c, h, half, 0).start()
            weights(c, h, half, 1).start()

        @pl.when(c == 1)
        def _():
            @pl.when(g == 1)
            def _():
                for k, (dx, dz) in enumerate(metas):
                    landing = ((x + dx) % NX) * NZ + (z - dz + NZ) % NZ
                    d = meta_copy(k, dx, dz, landing)
                    d.wait_send()
                    d.wait_recv()
                for i in range(NX * NZ):
                    mt[i] = mr[i].T[:TOK]

            routes(st, m)

    def d1(p, st, c, g):
        q, d, h, half = pairing(c)
        ring = g % RING
        finish(t1.at[st, c, x], t1.at[st, c, xn], X1, g, c, dev(xn, y, z))
        rows = dot(a1[st], t1[st, c].reshape(NX * KD * TOK, 128)) * pr1[st]
        y1s[ring] = rows.astype(BF16).reshape(NY, PADD, 128)
        to_y(lambda yd: y1s.at[ring, yd], y1, st, c, g, Y1)
        y1[st, c, y] = y1s[ring, y]
        mine = t3.at[st, c, x, z]
        finish(mine, t3.at[st, c, x, d], Z3A + q, g, c, dev(x, y, d))
        finish(xin.at[2 * p + st, :, half_col(c, S1, 1 - half, H3)], t3.at[st, c, x, h], Z3A + 1 - q, g, c, dev(x, y, h))
        fwd = t3.at[st, c, x, h]
        rcopy(fwd, fwd, Z3B + q, g, c, dev(x, y, d)).start()

    def d2(p, st, c, g):
        q, d, h, half = pairing(c)
        ring = g % RING
        from_y(lambda yd: y1s.at[ring, yd], y1, st, c, g, Y1)
        rows = dot(pick_ref[...], y1[st, c].reshape(NY * PADD, 128)).astype(BF16)
        for k in range(KD):
            lo = 128 * k % H1
            zs[ring, 128 * k // H1, :, lo:lo + 128] = rows[k * BLK:(k + 1) * BLK]
        z1[st, c, z] = zs[ring, half]
        mine = z1.at[st, c, z]
        rcopy(mine, mine, Z1A + q, g, c, dev(x, y, d)).start()
        rcopy(zs.at[ring, 1 - half], mine, Z1A + 1 - q, g, c, dev(x, y, h)).start()
        finish(t3.at[st, c, x, h], t3.at[st, c, x, z2], Z3B + q, g, c, dev(x, y, d))
        rcopy(t3.at[st, c, x], t3.at[st, c, x], X3, g, c, dev(xn, y, z)).start()

        @pl.when(c == 0)
        def _():
            @pl.when(g == 0)
            def _():
                load(saved_ref, svd, 4).wait()

            factors(st, 2 * p + st)

    def d3(p, st, c, g):
        q, d, h, half = pairing(c)
        ring = g % RING
        finish(z1.at[st, c, z], z1.at[st, c, d], Z1A + q, g, c, dev(x, y, d))
        finish(zs.at[ring, 1 - half], z1.at[st, c, h], Z1A + 1 - q, g, c, dev(x, y, h))
        fwd = z1.at[st, c, h]
        rcopy(fwd, fwd, Z1F + q, g, c, dev(x, y, d)).start()
        finish(t3.at[st, c, x], t3.at[st, c, xn], X3, g, c, dev(xn, y, z))
        rows = dot(a3[st], t3[st, c].reshape(NX * NZ * TOK, H3)) * pr3[st]
        y3s[ring] = rows.astype(BF16).reshape(NY, BLK, H3)
        to_y(lambda yd: y3s.at[ring, yd], y3, st, c, g, Y3)
        y3[st, c, y] = y3s[ring, y]

    def d4(p, st, c, g):
        q, d, h, half = pairing(c)
        ring = g % RING
        finish(z1.at[st, c, h], z1.at[st, c, z2], Z1F + q, g, c, dev(x, y, d))
        from_y(lambda yd: y3s.at[ring, yd], y3, st, c, g, Y3)

        @pl.when((p == 0) & (st == 0))
        def _():
            for piece in range(2):
                w = weights(c, h, half, piece)
                w.wait_send()
                w.wait_recv()

        rows1, rows3 = z1[st, c].reshape(ROWS, H1), y3[st, c].reshape(ROWS, H3)
        m1 = dot_t(rows1, wd[:, half_col(c, 0, half, H1)])
        m3 = dot_t(rows3, wd[:, half_col(c, S1, half, H3)])
        o1, o3 = dot_t(rows1, wp[c, 0]), dot_t(rows3, wp[c, 1])

        @pl.when(c == 0)
        def _():
            acc1[st] = m1
            acc3[st] = m3

        @pl.when(c > 0)
        def _():
            acc1[st] += m1
            acc3[st] += m3

        @pl.when(c < 2)
        def _():
            accp[st, q, 0] = o1
            accp[st, q, 1] = o3

        @pl.when(c >= 2)
        def _():
            accp[st, q, 0] += o1
            accp[st, q, 1] += o3

        @pl.when(c >= NCH - 2)
        def _():
            hs[q] = (accp[st, q, 0] + reorder(accp[st, q, 1])).astype(BF16)
            partials(st, q, h).start()

    def d5(p, st, c, g):
        q, d, h, half = pairing(c)

        @pl.when(c >= NCH - 2)
        def _():
            w = partials(st, q, h)
            w.wait_send()
            w.wait_recv()

        @pl.when(c == NCH - 1)
        def _():
            both = hr[st, 0].astype(F32) + hr[st, 1].astype(F32)
            h_all = acc1[st] + reorder(acc3[st]) + both
            gu1[st, :, 0:HD] = (h_all * fg[st]).astype(BF16)
            gu1[st, :, HD:2 * HD] = (h_all * fu[st]).astype(BF16)
            gu3[st] = dot(to3_ref[...], gu1[st]).astype(BF16)

    def r0(p, st, c, g):
        ring, deep = g % RING, g % DEEP

        @pl.when(g == 2 * NCH)
        def _():
            load(wg_ref, wgu.at[:, 0:HD], 6).wait()
            load(wu_ref, wgu.at[:, HD:2 * HD], 7).wait()

        part1 = dot_t(gu1[st], wgu[pl.ds(pl.multiple_of(c * CW, 128), C1), :])
        q1[deep] = part1.astype(BF16).reshape(NZ, BLK, C1)
        rcopy(q1.at[deep, z2, 0:HA], r1a.at[st, c, 0:HA], R1A, g, c, dev(x, y, za)).start()
        rcopy(q1.at[deep, z2, HA:BLK], r1a.at[st, c, HA:BLK], R1A + 1, g, c, dev(x, y, zb)).start()
        part3 = dot_t(gu3[st], wgu[pl.ds(pl.multiple_of(c * CW + C1, 128), C3), :])
        q3[ring] = part3.astype(BF16).reshape(NY, BLK, C3)
        to_y(lambda yd: q3.at[ring, yd], y3r, st, c, g, Y3R)
        y3r[st, c, y] = q3[ring, y]

    def r1(p, st, c, g):
        ring, deep = g % RING, g % DEEP
        finish(q1.at[deep, z2, 0:HA], r1a.at[st, c, 0:HA], R1A, g, c, dev(x, y, za))
        finish(q1.at[deep, z2, HA:BLK], r1a.at[st, c, HA:BLK], R1A + 1, g, c, dev(x, y, zb))
        s1[ring, 0, 0:HA] = (q1[deep, za, 0:HA].astype(F32) + r1a[st, c, 0:HA].astype(F32)).astype(BF16)
        s1[ring, 0, HA:BLK] = q1[deep, za, HA:BLK]
        rcopy(s1.at[ring, 0], r1b.at[st, c, 0], R1B, g, c, dev(x, y, za)).start()
        s1[ring, 1, 0:HA] = q1[deep, zb, 0:HA]
        s1[ring, 1, HA:BLK] = (q1[deep, zb, HA:BLK].astype(F32) + r1a[st, c, HA:BLK].astype(F32)).astype(BF16)
        rcopy(s1.at[ring, 1], r1b.at[st, c, 1], R1B + 1, g, c, dev(x, y, zb)).start()
        from_y(lambda yd: q3.at[ring, yd], y3r, st, c, g, Y3R)
        sums = dot(a3t[st], y3r[st, c].reshape(ROWS, C3))
        tb3[ring] = sums.astype(BF16).reshape(NX, NZ * TOK, C3)
        rcopy(tb3.at[ring, xn], x3r.at[st, c], X3R, g, c, dev(xn, y, z)).start()

    def r2(p, st, c, g):
        ring, deep = g % RING, g % DEEP
        finish(s1.at[ring, 0], r1b.at[st, c, 0], R1B, g, c, dev(x, y, za))
        finish(s1.at[ring, 1], r1b.at[st, c, 1], R1B + 1, g, c, dev(x, y, zb))
        total = q1[deep, z].astype(F32) + r1b[st, c, 0].astype(F32) + r1b[st, c, 1].astype(F32)
        total = total.astype(BF16)
        groups = jnp.concatenate([total[:, 128 * k:128 * (k + 1)] for k in range(KG)], axis=0)
        rows = dot(spread_ref[...], groups)
        y1rs[ring] = rows.astype(BF16).reshape(NY, PADY, 128)
        to_y(lambda yd: y1rs.at[ring, yd], y1rr, st, c, g, Y1R)
        y1rr[st, c, y] = y1rs[ring, y]
        finish(tb3.at[ring, xn], x3r.at[st, c], X3R, g, c, dev(xn, y, z))
        v = tb3[ring, x].astype(F32) + x3r[st, c].astype(F32)
        v3[deep] = v.astype(BF16).reshape(NZ, TOK, C3)
        rcopy(v3.at[deep, z2, 0:16], r3a.at[st, c, 0:16], R3A, g, c, dev(x, y, za)).start()
        rcopy(v3.at[deep, z2, 16:32], r3a.at[st, c, 16:32], R3A + 1, g, c, dev(x, y, zb)).start()

    def r3(p, st, c, g):
        ring, deep = g % RING, g % DEEP
        from_y(lambda yd: y1rs.at[ring, yd], y1rr, st, c, g, Y1R)
        sums = dot(a1t[st], y1rr[st, c].reshape(NY * PADY, 128))
        tb1[ring] = sums.astype(BF16).reshape(NX, KG, TOK, 128)
        rcopy(tb1.at[ring, xn], x1r.at[st, c], X1R, g, c, dev(xn, y, z)).start()
        finish(v3.at[deep, z2, 0:16], r3a.at[st, c, 0:16], R3A, g, c, dev(x, y, za))
        finish(v3.at[deep, z2, 16:32], r3a.at[st, c, 16:32], R3A + 1, g, c, dev(x, y, zb))
        s3[ring, 0, 0:16] = (v3[deep, za, 0:16].astype(F32) + r3a[st, c, 0:16].astype(F32)).astype(BF16)
        s3[ring, 0, 16:32] = v3[deep, za, 16:32]
        rcopy(s3.at[ring, 0], r3b.at[st, c, 0], R3B, g, c, dev(x, y, za)).start()
        s3[ring, 1, 0:16] = v3[deep, zb, 0:16]
        s3[ring, 1, 16:32] = (v3[deep, zb, 16:32].astype(F32) + r3a[st, c, 16:32].astype(F32)).astype(BF16)
        rcopy(s3.at[ring, 1], r3b.at[st, c, 1], R3B + 1, g, c, dev(x, y, zb)).start()

    def out_copy(m, c, ring):
        cols = col(c, 0, CW)
        return pltpu.make_async_copy(ob.at[m, :, cols], out_ref.at[m, :, cols], os.at[ring])

    def pipe_copy(m, st, c, g, to):
        cols = col(c, 0, CW)
        return rcopy(ob.at[m, :, cols], xin.at[m + 2, :, cols], PIPE + st, g, c, {"pipe": to})

    def r4(p, st, c, g):
        ring, deep = g % RING, g % DEEP
        m = 2 * p + st
        finish(tb1.at[ring, xn], x1r.at[st, c], X1R, g, c, dev(xn, y, z))
        finish(s3.at[ring, 0], r3b.at[st, c, 0], R3B, g, c, dev(x, y, za))
        finish(s3.at[ring, 1], r3b.at[st, c, 1], R3B + 1, g, c, dev(x, y, zb))
        for k in range(KG):
            cols = col(c, 128 * k, 128)
            o1 = xin[m, :, cols].astype(F32) + (tb1[ring, x, k].astype(F32) + x1r[st, c, k].astype(F32))
            ob[m, :, cols] = o1.astype(BF16)
        cols3 = col(c, C1, C3)
        o3 = xin[m, :, cols3].astype(F32) + (
            v3[deep, z].astype(F32) + r3b[st, c, 0].astype(F32) + r3b[st, c, 1].astype(F32)
        )
        ob[m, :, cols3] = o3.astype(BF16)
        out_copy(m, c, ring).start()

        @pl.when((p == 0) & (st == 0) & (pp > 0))
        def _():
            pipe_copy(0, 0, c, g, pp - 1).start()

        @pl.when((p == 0) & (st == 1) & (pp < 3))
        def _():
            pipe_copy(1, 1, c, g, pp + 1).start()

    def r5(p, st, c, g):
        out_copy(2 * p + st, c, g % RING).wait()

        @pl.when((p == 0) & (st == 0) & (pp > 0))
        def _():
            pipe_copy(0, 0, c, g, pp - 1).wait_send()

        @pl.when((p == 0) & (st == 1) & (pp < 3))
        def _():
            pipe_copy(1, 1, c, g, pp + 1).wait_send()

    def stage(t, k, returning, body):
        g = jnp.maximum(t - k, 0)
        p, w = g // SLOTS_PHASE, g % SLOTS_PHASE
        inside = (t - k >= 0) & (t - k < UNITS)
        here = (w >= 2 * NCH) if returning else (w < 2 * NCH)

        @pl.when(inside & here)
        def _():
            body(p, (w // NCH) % 2, w % NCH, g)

    def tick(t, carry):
        for k, body in zip(DISPATCH, [d0, d1, d2, d3, d4, d5]):
            stage(t, k, False, body)
        for k, body in zip(RETURN, [r0, r1, r2, r3, r4, r5]):
            stage(t, k, True, body)
        return carry

    lax.fori_loop(0, UNITS + RETURN[-1], tick, 0)


def layers(xa, xb, na, nb, meta, saved, wg, wu, wdn):
    consts = [jnp.asarray(a) for a in constants()]
    any_spec = pl.BlockSpec(memory_space=pl.ANY)
    vmem = pl.BlockSpec(memory_space=pltpu.VMEM)
    V = pltpu.VMEM
    scratch = [
        V((4, TOK, D), BF16),
        V((4, TOK, D), BF16),
        V((D, 2 * HD), BF16),
        V((HD, D), BF16),
        V((4, 2 * ROWS, HD), BF16),
        V((NX * NZ, 32, 128), F32),
        V((NX * NZ, TOK, TOK), F32),
        V((2, NY * PADD, NX * KD * TOK), BF16),
        V((2, NX * KG * TOK, NY * PADY), BF16),
        V((2, NY * PADD, 1), F32),
        V((2, ROWS, NX * NZ * TOK), BF16),
        V((2, NX * NZ * TOK, ROWS), BF16),
        V((2, ROWS, 1), F32),
        V((2, ROWS, HD), F32),
        V((2, ROWS, HD), F32),
        V((2, ROWS, HD), F32),
        V((2, ROWS, HD), F32),
        V((2, 2, 2, ROWS, HD), F32),
        V((2, ROWS, 2 * HD), BF16),
        V((2, ROWS, 2 * HD), BF16),
        V((2, NCH, NX, KD, TOK, 128), BF16),
        V((2, NCH, NY, PADD, 128), BF16),
        V((2, NCH, NZ, BLK, H1), BF16),
        V((2, NCH, NX, NZ, TOK, H3), BF16),
        V((2, NCH, NY, BLK, H3), BF16),
        V((RING, NY, PADD, 128), BF16),
        V((RING, NY, BLK, H3), BF16),
        V((RING, 2, BLK, H1), BF16),
        V((NCH, 2, HD, H1), BF16),
        V((2, ROWS, HD), BF16),
        V((2, 2, ROWS, HD), BF16),
        V((DEEP, NZ, BLK, C1), BF16),
        V((RING, 2, BLK, C1), BF16),
        V((2, NCH, BLK, C1), BF16),
        V((2, NCH, 2, BLK, C1), BF16),
        V((RING, NY, PADY, 128), BF16),
        V((2, NCH, NY, PADY, 128), BF16),
        V((RING, NX, KG, TOK, 128), BF16),
        V((2, NCH, KG, TOK, 128), BF16),
        V((RING, NY, BLK, C3), BF16),
        V((2, NCH, NY, BLK, C3), BF16),
        V((RING, NX, NZ * TOK, C3), BF16),
        V((2, NCH, NZ * TOK, C3), BF16),
        V((DEEP, NZ, TOK, C3), BF16),
        V((RING, 2, TOK, C3), BF16),
        V((2, NCH, TOK, C3), BF16),
        V((2, NCH, 2, TOK, C3), BF16),
        pltpu.SemaphoreType.DMA((RING, KINDS)),
        pltpu.SemaphoreType.DMA((NCH, KINDS)),
        pltpu.SemaphoreType.DMA((8,)),
        pltpu.SemaphoreType.DMA((8,)),
        pltpu.SemaphoreType.DMA((8,)),
        pltpu.SemaphoreType.DMA((RING,)),
        pltpu.SemaphoreType.DMA((NCH, 2)),
        pltpu.SemaphoreType.DMA((NCH, 2)),
        pltpu.SemaphoreType.DMA((2,)),
        pltpu.SemaphoreType.DMA((2, 2)),
    ]
    flops = 4 * 2 * ROWS * D * HD * 3
    return pl.pallas_call(
        kernel,
        out_shape=jax.ShapeDtypeStruct((4, TOK, D), BF16),
        in_specs=[any_spec] * 4 + [vmem] + [any_spec] * 4 + [vmem] * len(consts),
        out_specs=any_spec,
        scratch_shapes=scratch,
        compiler_params=pltpu.CompilerParams(
            collective_id=0, has_side_effects=True, vmem_limit_bytes=63 * 2**20
        ),
        cost_estimate=pl.CostEstimate(flops=flops, bytes_accessed=16 * 2**20, transcendentals=0),
        name="relay_layers",
    )(xa, xb, na, nb, meta, saved, wg, wu, wdn, *consts)


def route_data(ids, probs):
    micro = ids.shape[0]
    flat = ids.reshape(micro, TOK * TOPK)
    pair = jnp.arange(TOK * TOPK)
    earlier = (flat[:, :, None] == flat[:, None, :]) & (pair[None, :] < pair[:, None])
    ranking = jnp.sum(earlier.astype(jnp.int32), axis=2)
    slots = (flat * CAP + ranking).reshape(micro, TOK, TOPK).astype(F32)
    both = jnp.concatenate([slots, probs], axis=2)
    by_row = jnp.tile(both.transpose(0, 2, 1), (1, 2, 128 // TOK))
    return by_row.reshape(micro * 8, 128)


def per_device(
    held_a, held_b, new_a, new_b, expert_ids, route_probs, saved_gate_up, w_gate, w_up, w_down
):
    meta = route_data(expert_ids[0], route_probs[0])
    saved = saved_gate_up[0].reshape(4, 2 * ROWS, HD)
    out = layers(
        held_a[0], held_b[0], new_a, new_b, meta, saved, w_gate[0], w_up[0], w_down[0]
    )
    return out[0][None], out[1][None], out[2][None], out[3][None]


def solution(mesh):
    in_specs = (
        P("pipe", "expert", None),
        P("pipe", "expert", None),
        P("expert", None),
        P("expert", None),
        P("pipe", None, "expert", None),
        P("pipe", None, "expert", None),
        P("pipe", None, None, None, "expert"),
        P("pipe", None, "expert"),
        P("pipe", None, "expert"),
        P("pipe", "expert", None),
    )
    out_specs = (P("pipe", "expert", None),) * 4
    return jax.shard_map(
        per_device, mesh=mesh, in_specs=in_specs, out_specs=out_specs, check_vma=False
    )
```

```python
import functools

import jax
import jax.numpy as jnp
import numpy as np
from jax import lax
from jax.experimental import pallas as pl
from jax.experimental.pallas import tpu as pltpu
from jax.sharding import PartitionSpec as P

EXPERTS = 8
TOPK = 2
CAP = 10
D = 7168
TOK = 32
HD = 256
NX, NY, NZ = 2, 4, 4
ROWS = NX * NY * NZ * CAP
BLK = ROWS // 4
RUN = NX * CAP
NCH = 7
CW = D // NCH
C1 = 640
C3 = CW - C1
KG = C1 // 128
PADY = -(-KG * RUN // 16) * 16
HA = 48
S1 = 512
S3 = CW - S1
KD = S1 // 128
PADD = -(-KD * RUN // 16) * 16
H1, H3 = S1 // 2, S3 // 2
GAP = 2
DISPATCH = (0, 2, 4, 6, 8, 10)
RETURN = (2, 4, 6, 8, 10, 12)
RING = GAP + 1
DEEP = 2 * GAP + 1
SLOTS_PHASE = 4 * NCH
UNITS = 2 * SLOTS_PHASE
MESH = pl.DeviceIdType.MESH
F32, BF16 = jnp.float32, jnp.bfloat16

X1, Y1, Z3A, Z3B, Z1A, Z1F, X3, Y3 = 0, 1, 4, 6, 8, 10, 12, 13
R1A, Y3R, R1B, X3R, Y1R, R3A, X1R, R3B, PIPE = 16, 18, 21, 23, 24, 27, 29, 30, 32
KINDS = 34


def constants():
    c = np.arange(CAP)
    order1 = np.array(
        [(x, y, z, k) for z in range(NZ) for y in range(NY) for x in range(NX) for k in c]
    )
    order3 = np.array(
        [(x, y, z, k) for y in range(NY) for x in range(NX) for z in range(NZ) for k in c]
    )
    row = lambda o: ((o[:, 0] * NY + o[:, 1]) * NZ + o[:, 2]) * CAP + o[:, 3]
    row1, row3 = row(order1), row(order3)
    from3 = (row1[:, None] == row3[None, :]).astype(np.float32)
    from_saved = np.concatenate(
        [(2 * row1 + i)[:, None] == np.arange(2 * ROWS)[None, :] for i in range(2)], axis=0
    )
    want3 = (order3[:, 0] * NZ + order3[:, 2]) * 128 + order3[:, 1] * CAP + order3[:, 3]

    def stacked(groups, pad):
        want = np.full((NY * pad,), -(1 << 20))
        pick = np.zeros((groups * BLK, NY * pad), np.float32)
        for y in range(NY):
            for group in range(groups):
                for r in range(RUN):
                    i = y * pad + group * RUN + r
                    want[i] = group * 1024 + (r // CAP) * 128 + y * CAP + r % CAP
                    pick[group * BLK + y * RUN + r, i] = 1
        off = [k * 1024 + x * 128 for x in range(NX) for k in range(groups) for t in range(TOK)]
        return want, pick, np.array(off)

    want1, pick1, off1 = stacked(KD, PADD)
    want1r, pick1r, off1r = stacked(KG, PADY)
    lane = np.zeros((1, 128), np.float32)
    lane[0] = np.arange(128) // TOK
    off3 = (np.arange(NX * NZ * TOK) // TOK) * 128
    f = lambda a: np.asarray(a, np.float32)
    b = lambda a: np.asarray(a, np.float32).astype(jnp.bfloat16)
    return (
        b(from3),
        b(from3.T),
        b(from_saved),
        b(pick1),
        b(pick1r.T),
        f(want3)[:, None],
        f(want3)[None, :],
        f(want1)[:, None],
        f(want1r)[None, :],
        f(off3)[:, None],
        f(off3)[None, :],
        f(off1r)[:, None],
        f(off1)[None, :],
        lane,
    )


def dot(a, b):
    return lax.dot_general(a, b, (((1,), (0,)), ((), ())), preferred_element_type=F32)


def dot_t(a, b):
    return lax.dot_general(a, b, (((1,), (1,)), ((), ())), preferred_element_type=F32)


def kernel(
    xa_ref, xb_ref, na_ref, nb_ref, ids_ref, probs_ref, saved_ref, wg_ref, wu_ref, wdn_ref,
    from3_ref, to3_ref, froms_ref, pick_ref, spread_ref,
    w3c_ref, w3r_ref, w1c_ref, w1r_ref, o3c_ref, o3r_ref, o1c_ref, o1r_ref, lane_ref,
    out_ref,
    xin, ob, wgu, wd, svd, mr, mt, mb, a1, a1t, pr1, a3, a3t, pr3, fg, fu, acc1, acc3, accp, gu1, gu3,
    t1, y1, z1, t3, y3, y1s, y3s, zs, wp, hs, hr,
    q1, s1, r1a, r1b, y1rs, y1rr, tb1, x1r, q3, y3r, tb3, x3r, v3, s3, r3a, r3b,
    ss, rs, mss, mrs, ls, os, wss, wrs, hss, hrs,
):
    me = lax.axis_index("expert")
    pp = lax.axis_index("pipe")
    x, y, z = me // (NY * NZ), (me // NZ) % NY, me % NZ
    core = pp % 2
    xn = 1 - x
    za = (z + 1 + 2 * core) % NZ
    zb = (z + 3 - 2 * core) % NZ
    z2 = (z + 2) % NZ
    near1, near2 = z + 1 - 2 * (z % 2), 3 - z

    def pairing(c):
        q = c % 2
        d = jnp.where(q == 0, near1, near2)
        h = jnp.where(q == 0, near2, near1)
        return q, d, h, jnp.where(q == 0, z // 2, ((z + 1) // 2) % 2)

    def dev(px, py, pz):
        return {"expert": (px * NY + py) * NZ + pz}

    def rcopy(src, dst, kind, g, c, to):
        return pltpu.make_async_remote_copy(
            src_ref=src, dst_ref=dst, send_sem=ss.at[g % RING, kind], recv_sem=rs.at[c, kind],
            device_id=to, device_id_type=MESH,
        )

    def finish(src, landing, kind, g, c, to):
        d = rcopy(src, landing, kind, g, c, to)
        d.wait_send()
        d.wait_recv()

    def load(src, dst, k):
        return pltpu.make_async_copy(src, dst, ls.at[k])

    load(xa_ref, xin.at[0], 0).start()
    load(xb_ref, xin.at[1], 1).start()

    @pl.when(pp == 3)
    def _():
        load(na_ref, xin.at[2], 2).start()

    @pl.when(pp == 0)
    def _():
        load(nb_ref, xin.at[3], 3).start()

    load(saved_ref, svd, 4).start()
    load(wdn_ref, wd, 5).start()
    load(wg_ref, wgu.at[:, 0:HD], 6).start()
    load(wu_ref, wgu.at[:, HD:2 * HD], 7).start()

    before = lax.broadcasted_iota(jnp.int32, (TOK, TOK), 0) < lax.broadcasted_iota(jnp.int32, (TOK, TOK), 1)
    before = jnp.where(before, 1.0, 0.0).astype(BF16)
    expert = lax.broadcasted_iota(jnp.int32, (EXPERTS, TOK), 0).astype(F32)
    mb[...] = jnp.zeros_like(mb)
    for m in range(4):
        ids = ids_ref[m].astype(F32)
        named = [expert == ids[k:k + 1] for k in range(TOPK)]
        count = jnp.where(named[0], 1.0, 0.0) + jnp.where(named[1], 1.0, 0.0)
        earlier = dot(count.astype(BF16), before)
        for k in range(TOPK):
            rank = jnp.sum(jnp.where(named[k], earlier, 0.0), axis=0, keepdims=True)
            mb[m * 8 + k:m * 8 + k + 1, 0:TOK] = ids[k:k + 1] * float(CAP) + rank
        mb[m * 8 + 2:m * 8 + 4, 0:TOK] = probs_ref[m]
    tile = mb[...]
    tile = tile + pltpu.roll(tile, TOK, 1)
    mb[...] = tile + pltpu.roll(tile, 2 * TOK, 1)

    barrier = pltpu.get_barrier_semaphore()
    metas = [(dx, dz) for dx in range(NX) for dz in range(NZ) if dx or dz]
    for dx, dz in metas:
        pl.semaphore_signal(barrier, 1, device_id=dev((x + dx) % NX, y, (z + dz) % NZ), device_id_type=MESH)
    for dy in range(1, NY):
        pl.semaphore_signal(barrier, 1, device_id=dev(x, (y + dy) % NY, z), device_id_type=MESH)

    @pl.when(pp > 0)
    def _():
        pl.semaphore_signal(barrier, 1, device_id={"pipe": pp - 1}, device_id_type=MESH)

    @pl.when(pp < 3)
    def _():
        pl.semaphore_signal(barrier, 1, device_id={"pipe": pp + 1}, device_id_type=MESH)

    in_pipe = jnp.where((pp == 0) | (pp == 3), 1, 2)
    pl.semaphore_wait(barrier, len(metas) + NY - 1 + in_pipe)

    src_me = x * NZ + z
    mr[src_me] = mb[...]

    def meta_copy(k, dx, dz, landing):
        return pltpu.make_async_remote_copy(
            src_ref=mb, dst_ref=mr.at[landing], send_sem=mss.at[k], recv_sem=mrs.at[k],
            device_id=dev((x + dx) % NX, y, (z + dz) % NZ), device_id_type=MESH,
        )

    for k, (dx, dz) in enumerate(metas):
        meta_copy(k, dx, dz, src_me).start()

    load(xa_ref, xin.at[0], 0).wait()
    load(xb_ref, xin.at[1], 1).wait()

    @pl.when(pp == 3)
    def _():
        load(na_ref, xin.at[2], 2).wait()

    @pl.when(pp == 0)
    def _():
        load(nb_ref, xin.at[3], 3).wait()

    def col(c, off, width):
        return pl.ds(pl.multiple_of(c * CW + off, 128), width)

    def routes(st, m):
        lane = lane_ref[...]

        def rowpart(s):
            return mr[s, pl.ds(pl.multiple_of(m * 8, 8), 8), :]

        def lanes(parts):
            r = parts[-1]
            for i in range(len(parts) - 2, -1, -1):
                r = jnp.where(lane == float(i), parts[i], r)
            return r

        lane_no = lax.broadcasted_iota(jnp.int32, (1, TOK), 1)

        def column(arr, k):
            return jnp.sum(jnp.where(lane_no == m * 8 + k, arr, 0.0), axis=1, keepdims=True)

        mine = (x * 40).astype(F32)
        near, far = rowpart(z), rowpart(NZ + z)
        r1 = jnp.concatenate([near, far], axis=1)
        o1 = o1r_ref[...]
        w1 = w1c_ref[...] + mine
        h0, h1 = w1 == r1[0:1] + o1, w1 == r1[1:2] + o1
        a1[st] = jnp.where(h0 | h1, 1.0, 0.0).astype(BF16)
        pr1[st] = jnp.sum(jnp.where(h0, r1[2:3], 0.0) + jnp.where(h1, r1[3:4], 0.0), axis=1, keepdims=True)
        c1 = jnp.concatenate([mt[z]] * KG + [mt[NZ + z]] * KG, axis=0)
        o1c = o1c_ref[...]
        w1t = w1r_ref[...] + mine
        a1t[st] = jnp.where(
            (column(c1, 0) + o1c == w1t) | (column(c1, 1) + o1c == w1t), 1.0, 0.0
        ).astype(BF16)
        r3 = jnp.concatenate([lanes([rowpart(s) for s in range(4)]), lanes([rowpart(s) for s in range(4, 8)])], axis=1)
        o3 = o3r_ref[...]
        w3 = w3c_ref[...] + mine
        h0, h1 = w3 == r3[0:1] + o3, w3 == r3[1:2] + o3
        a3[st] = jnp.where(h0 | h1, 1.0, 0.0).astype(BF16)
        pr3[st] = jnp.sum(jnp.where(h0, r3[2:3], 0.0) + jnp.where(h1, r3[3:4], 0.0), axis=1, keepdims=True)
        c3 = mt[...].reshape(NX * NZ * TOK, TOK)
        o3t = o3c_ref[...]
        w3t = w3r_ref[...] + mine
        a3t[st] = jnp.where(
            (column(c3, 0) + o3t == w3t) | (column(c3, 1) + o3t == w3t), 1.0, 0.0
        ).astype(BF16)

    def factors(st, m):
        gu = dot(froms_ref[...], svd[m].reshape(2 * ROWS, HD))
        gate, up = gu[:ROWS], gu[ROWS:]
        sig = jax.nn.sigmoid(gate)
        fg[st] = up * sig * (1.0 + gate * (1.0 - sig))
        fu[st] = gate * sig

    def to_y(src_of, buf, st, c, g, kind):
        for dy in range(1, NY):
            yd = (y + dy) % NY
            rcopy(src_of(yd), buf.at[st, c, y], kind + dy - 1, g, c, dev(x, yd, z)).start()

    def from_y(src_of, buf, st, c, g, kind):
        for dy in range(1, NY):
            yd, ys = (y + dy) % NY, (y - dy + NY) % NY
            finish(src_of(yd), buf.at[st, c, ys], kind + dy - 1, g, c, dev(x, yd, z))

    def half_col(c, off, half, width):
        return pl.ds(pl.multiple_of(c * CW + off + half * width, 128), width)

    def weights(c, h, half, piece):
        cols = half_col(c, piece * S1, 1 - half, H1)
        return pltpu.make_async_remote_copy(
            src_ref=wd.at[:, cols], dst_ref=wp.at[c, piece], send_sem=wss.at[c, piece],
            recv_sem=wrs.at[c, piece], device_id=dev(x, y, h), device_id_type=MESH,
        )

    def partials(st, q, h):
        return pltpu.make_async_remote_copy(
            src_ref=hs.at[q], dst_ref=hr.at[st, q], send_sem=hss.at[q],
            recv_sem=hrs.at[st, q], device_id=dev(x, y, h), device_id_type=MESH,
        )

    def reorder(a):
        high = a.astype(BF16)
        low = (a - high.astype(F32)).astype(BF16)
        return dot(from3_ref[...], high) + dot(from3_ref[...], low)

    def d0(p, st, c, g):
        m = 2 * p + st

        @pl.when((p == 1) & (((st == 0) & (pp < 3)) | ((st == 1) & (pp > 0))))
        def _():
            landing = xin.at[m, :, col(c, 0, CW)]
            rcopy(landing, landing, PIPE + st, g, c, {"pipe": pp}).wait_recv()

        q, d, h, half = pairing(c)
        for k in range(KD):
            t1[st, c, x, k] = xin[m, :, col(c, 128 * k, 128)]
        rcopy(t1.at[st, c, x], t1.at[st, c, x], X1, g, c, dev(xn, y, z)).start()
        t3[st, c, x, z] = xin[m, :, half_col(c, S1, half, H3)]
        mine = t3.at[st, c, x, z]
        rcopy(mine, mine, Z3A + q, g, c, dev(x, y, d)).start()
        rcopy(xin.at[m, :, half_col(c, S1, 1 - half, H3)], mine, Z3A + 1 - q, g, c, dev(x, y, h)).start()

        @pl.when(g == 0)
        def _():
            load(wdn_ref, wd, 5).wait()

        first = (4 * g + 2) // 3
        for i in range(2):
            now = first + i

            @pl.when((now < 2 * NCH) & ((3 * now) // 4 == g))
            def _():
                _, _, other, side = pairing(now // 2)
                cols = half_col(now // 2, (now % 2) * S1, 1 - side, H1)
                pltpu.make_async_remote_copy(
                    src_ref=wd.at[:, cols], dst_ref=wp.at[now // 2, now % 2],
                    send_sem=wss.at[now // 2, now % 2], recv_sem=wrs.at[now // 2, now % 2],
                    device_id=dev(x, y, other), device_id_type=MESH,
                ).start()


        @pl.when(c == 1)
        def _():
            @pl.when(g == 1)
            def _():
                for k, (dx, dz) in enumerate(metas):
                    landing = ((x + dx) % NX) * NZ + (z - dz + NZ) % NZ
                    d = meta_copy(k, dx, dz, landing)
                    d.wait_send()
                    d.wait_recv()
                for i in range(NX * NZ):
                    mt[i] = mr[i].T[:TOK]

            routes(st, m)

    def d1(p, st, c, g):
        q, d, h, half = pairing(c)
        ring = g % RING
        finish(t1.at[st, c, x], t1.at[st, c, xn], X1, g, c, dev(xn, y, z))
        rows = dot(a1[st], t1[st, c].reshape(NX * KD * TOK, 128)) * pr1[st]
        y1s[ring] = rows.astype(BF16).reshape(NY, PADD, 128)
        to_y(lambda yd: y1s.at[ring, yd], y1, st, c, g, Y1)
        y1[st, c, y] = y1s[ring, y]
        mine = t3.at[st, c, x, z]
        finish(mine, t3.at[st, c, x, d], Z3A + q, g, c, dev(x, y, d))
        finish(xin.at[2 * p + st, :, half_col(c, S1, 1 - half, H3)], t3.at[st, c, x, h], Z3A + 1 - q, g, c, dev(x, y, h))
        fwd = t3.at[st, c, x, h]
        rcopy(fwd, fwd, Z3B + q, g, c, dev(x, y, d)).start()

    def d2(p, st, c, g):
        q, d, h, half = pairing(c)
        ring = g % RING
        from_y(lambda yd: y1s.at[ring, yd], y1, st, c, g, Y1)
        rows = dot(pick_ref[...], y1[st, c].reshape(NY * PADD, 128)).astype(BF16)
        for k in range(KD):
            lo = 128 * k % H1
            zs[ring, 128 * k // H1, :, lo:lo + 128] = rows[k * BLK:(k + 1) * BLK]
        z1[st, c, z] = zs[ring, half]
        mine = z1.at[st, c, z]
        rcopy(mine, mine, Z1A + q, g, c, dev(x, y, d)).start()
        rcopy(zs.at[ring, 1 - half], mine, Z1A + 1 - q, g, c, dev(x, y, h)).start()
        finish(t3.at[st, c, x, h], t3.at[st, c, x, z2], Z3B + q, g, c, dev(x, y, d))
        rcopy(t3.at[st, c, x], t3.at[st, c, x], X3, g, c, dev(xn, y, z)).start()

        @pl.when(c == 0)
        def _():
            @pl.when(g == 0)
            def _():
                load(saved_ref, svd, 4).wait()

            factors(st, 2 * p + st)

    def d3(p, st, c, g):
        q, d, h, half = pairing(c)
        ring = g % RING
        finish(z1.at[st, c, z], z1.at[st, c, d], Z1A + q, g, c, dev(x, y, d))
        finish(zs.at[ring, 1 - half], z1.at[st, c, h], Z1A + 1 - q, g, c, dev(x, y, h))
        fwd = z1.at[st, c, h]
        rcopy(fwd, fwd, Z1F + q, g, c, dev(x, y, d)).start()
        finish(t3.at[st, c, x], t3.at[st, c, xn], X3, g, c, dev(xn, y, z))
        rows = dot(a3[st], t3[st, c].reshape(NX * NZ * TOK, H3)) * pr3[st]
        y3s[ring] = rows.astype(BF16).reshape(NY, BLK, H3)
        to_y(lambda yd: y3s.at[ring, yd], y3, st, c, g, Y3)
        y3[st, c, y] = y3s[ring, y]

    def d4(p, st, c, g):
        q, d, h, half = pairing(c)
        ring = g % RING
        finish(z1.at[st, c, h], z1.at[st, c, z2], Z1F + q, g, c, dev(x, y, d))
        from_y(lambda yd: y3s.at[ring, yd], y3, st, c, g, Y3)

        @pl.when((p == 0) & (st == 0))
        def _():
            for piece in range(2):
                w = weights(c, h, half, piece)
                w.wait_send()
                w.wait_recv()

        rows1, rows3 = z1[st, c].reshape(ROWS, H1), y3[st, c].reshape(ROWS, H3)
        m1 = dot_t(rows1, wd[:, half_col(c, 0, half, H1)])
        m3 = dot_t(rows3, wd[:, half_col(c, S1, half, H3)])
        o1, o3 = dot_t(rows1, wp[c, 0]), dot_t(rows3, wp[c, 1])

        @pl.when(c == 0)
        def _():
            acc1[st] = m1
            acc3[st] = m3

        @pl.when(c > 0)
        def _():
            acc1[st] += m1
            acc3[st] += m3

        @pl.when(c < 2)
        def _():
            accp[st, q, 0] = o1
            accp[st, q, 1] = o3

        @pl.when(c >= 2)
        def _():
            accp[st, q, 0] += o1
            accp[st, q, 1] += o3

        @pl.when(c >= NCH - 2)
        def _():
            hs[q] = (accp[st, q, 0] + reorder(accp[st, q, 1])).astype(BF16)
            partials(st, q, h).start()

    def d5(p, st, c, g):
        q, d, h, half = pairing(c)

        @pl.when(c >= NCH - 2)
        def _():
            w = partials(st, q, h)
            w.wait_send()
            w.wait_recv()

        @pl.when(c == NCH - 1)
        def _():
            both = hr[st, 0].astype(F32) + hr[st, 1].astype(F32)
            h_all = acc1[st] + reorder(acc3[st]) + both
            gu1[st, :, 0:HD] = (h_all * fg[st]).astype(BF16)
            gu1[st, :, HD:2 * HD] = (h_all * fu[st]).astype(BF16)
            gu3[st] = dot(to3_ref[...], gu1[st]).astype(BF16)

    def r0(p, st, c, g):
        ring, deep = g % RING, g % DEEP

        @pl.when(g == 2 * NCH)
        def _():
            load(wg_ref, wgu.at[:, 0:HD], 6).wait()
            load(wu_ref, wgu.at[:, HD:2 * HD], 7).wait()

        part1 = dot_t(gu1[st], wgu[pl.ds(pl.multiple_of(c * CW, 128), C1), :])
        q1[deep] = part1.astype(BF16).reshape(NZ, BLK, C1)
        rcopy(q1.at[deep, z2, 0:HA], r1a.at[st, c, 0:HA], R1A, g, c, dev(x, y, za)).start()
        rcopy(q1.at[deep, z2, HA:BLK], r1a.at[st, c, HA:BLK], R1A + 1, g, c, dev(x, y, zb)).start()
        part3 = dot_t(gu3[st], wgu[pl.ds(pl.multiple_of(c * CW + C1, 128), C3), :])
        q3[ring] = part3.astype(BF16).reshape(NY, BLK, C3)
        to_y(lambda yd: q3.at[ring, yd], y3r, st, c, g, Y3R)
        y3r[st, c, y] = q3[ring, y]

    def r1(p, st, c, g):
        ring, deep = g % RING, g % DEEP
        finish(q1.at[deep, z2, 0:HA], r1a.at[st, c, 0:HA], R1A, g, c, dev(x, y, za))
        finish(q1.at[deep, z2, HA:BLK], r1a.at[st, c, HA:BLK], R1A + 1, g, c, dev(x, y, zb))
        s1[ring, 0, 0:HA] = (q1[deep, za, 0:HA].astype(F32) + r1a[st, c, 0:HA].astype(F32)).astype(BF16)
        s1[ring, 0, HA:BLK] = q1[deep, za, HA:BLK]
        rcopy(s1.at[ring, 0], r1b.at[st, c, 0], R1B, g, c, dev(x, y, za)).start()
        s1[ring, 1, 0:HA] = q1[deep, zb, 0:HA]
        s1[ring, 1, HA:BLK] = (q1[deep, zb, HA:BLK].astype(F32) + r1a[st, c, HA:BLK].astype(F32)).astype(BF16)
        rcopy(s1.at[ring, 1], r1b.at[st, c, 1], R1B + 1, g, c, dev(x, y, zb)).start()
        from_y(lambda yd: q3.at[ring, yd], y3r, st, c, g, Y3R)
        sums = dot(a3t[st], y3r[st, c].reshape(ROWS, C3))
        tb3[ring] = sums.astype(BF16).reshape(NX, NZ * TOK, C3)
        rcopy(tb3.at[ring, xn], x3r.at[st, c], X3R, g, c, dev(xn, y, z)).start()

    def r2(p, st, c, g):
        ring, deep = g % RING, g % DEEP
        finish(s1.at[ring, 0], r1b.at[st, c, 0], R1B, g, c, dev(x, y, za))
        finish(s1.at[ring, 1], r1b.at[st, c, 1], R1B + 1, g, c, dev(x, y, zb))
        total = q1[deep, z].astype(F32) + r1b[st, c, 0].astype(F32) + r1b[st, c, 1].astype(F32)
        total = total.astype(BF16)
        groups = jnp.concatenate([total[:, 128 * k:128 * (k + 1)] for k in range(KG)], axis=0)
        rows = dot(spread_ref[...], groups)
        y1rs[ring] = rows.astype(BF16).reshape(NY, PADY, 128)
        to_y(lambda yd: y1rs.at[ring, yd], y1rr, st, c, g, Y1R)
        y1rr[st, c, y] = y1rs[ring, y]
        finish(tb3.at[ring, xn], x3r.at[st, c], X3R, g, c, dev(xn, y, z))
        v = tb3[ring, x].astype(F32) + x3r[st, c].astype(F32)
        v3[deep] = v.astype(BF16).reshape(NZ, TOK, C3)
        rcopy(v3.at[deep, z2, 0:16], r3a.at[st, c, 0:16], R3A, g, c, dev(x, y, za)).start()
        rcopy(v3.at[deep, z2, 16:32], r3a.at[st, c, 16:32], R3A + 1, g, c, dev(x, y, zb)).start()

    def r3(p, st, c, g):
        ring, deep = g % RING, g % DEEP
        from_y(lambda yd: y1rs.at[ring, yd], y1rr, st, c, g, Y1R)
        sums = dot(a1t[st], y1rr[st, c].reshape(NY * PADY, 128))
        tb1[ring] = sums.astype(BF16).reshape(NX, KG, TOK, 128)
        rcopy(tb1.at[ring, xn], x1r.at[st, c], X1R, g, c, dev(xn, y, z)).start()
        finish(v3.at[deep, z2, 0:16], r3a.at[st, c, 0:16], R3A, g, c, dev(x, y, za))
        finish(v3.at[deep, z2, 16:32], r3a.at[st, c, 16:32], R3A + 1, g, c, dev(x, y, zb))
        s3[ring, 0, 0:16] = (v3[deep, za, 0:16].astype(F32) + r3a[st, c, 0:16].astype(F32)).astype(BF16)
        s3[ring, 0, 16:32] = v3[deep, za, 16:32]
        rcopy(s3.at[ring, 0], r3b.at[st, c, 0], R3B, g, c, dev(x, y, za)).start()
        s3[ring, 1, 0:16] = v3[deep, zb, 0:16]
        s3[ring, 1, 16:32] = (v3[deep, zb, 16:32].astype(F32) + r3a[st, c, 16:32].astype(F32)).astype(BF16)
        rcopy(s3.at[ring, 1], r3b.at[st, c, 1], R3B + 1, g, c, dev(x, y, zb)).start()

    def out_copy(m, c, ring):
        cols = col(c, 0, CW)
        return pltpu.make_async_copy(ob.at[m, :, cols], out_ref.at[m, :, cols], os.at[ring])

    def pipe_copy(m, st, c, g, to):
        cols = col(c, 0, CW)
        return rcopy(ob.at[m, :, cols], xin.at[m + 2, :, cols], PIPE + st, g, c, {"pipe": to})

    def r4(p, st, c, g):
        ring, deep = g % RING, g % DEEP
        m = 2 * p + st
        finish(tb1.at[ring, xn], x1r.at[st, c], X1R, g, c, dev(xn, y, z))
        finish(s3.at[ring, 0], r3b.at[st, c, 0], R3B, g, c, dev(x, y, za))
        finish(s3.at[ring, 1], r3b.at[st, c, 1], R3B + 1, g, c, dev(x, y, zb))
        for k in range(KG):
            cols = col(c, 128 * k, 128)
            o1 = xin[m, :, cols].astype(F32) + (tb1[ring, x, k].astype(F32) + x1r[st, c, k].astype(F32))
            ob[m, :, cols] = o1.astype(BF16)
        cols3 = col(c, C1, C3)
        o3 = xin[m, :, cols3].astype(F32) + (
            v3[deep, z].astype(F32) + r3b[st, c, 0].astype(F32) + r3b[st, c, 1].astype(F32)
        )
        ob[m, :, cols3] = o3.astype(BF16)
        out_copy(m, c, ring).start()

        @pl.when((p == 0) & (st == 0) & (pp > 0))
        def _():
            pipe_copy(0, 0, c, g, pp - 1).start()

        @pl.when((p == 0) & (st == 1) & (pp < 3))
        def _():
            pipe_copy(1, 1, c, g, pp + 1).start()

    def r5(p, st, c, g):
        out_copy(2 * p + st, c, g % RING).wait()

        @pl.when((p == 0) & (st == 0) & (pp > 0))
        def _():
            pipe_copy(0, 0, c, g, pp - 1).wait_send()

        @pl.when((p == 0) & (st == 1) & (pp < 3))
        def _():
            pipe_copy(1, 1, c, g, pp + 1).wait_send()

    def stage(t, k, returning, body):
        g = jnp.maximum(t - k, 0)
        p, w = g // SLOTS_PHASE, g % SLOTS_PHASE
        inside = (t - k >= 0) & (t - k < UNITS)
        here = (w >= 2 * NCH) if returning else (w < 2 * NCH)

        @pl.when(inside & here)
        def _():
            body(p, (w // NCH) % 2, w % NCH, g)

    def tick(t, carry):
        for k, body in zip(DISPATCH, [d0, d1, d2, d3, d4, d5]):
            stage(t, k, False, body)
        for k, body in zip(RETURN, [r0, r1, r2, r3, r4, r5]):
            stage(t, k, True, body)
        return carry

    lax.fori_loop(0, UNITS + RETURN[-1], tick, 0)


def layers(xa, xb, na, nb, ids, probs, saved, wg, wu, wdn):
    consts = [jnp.asarray(a) for a in constants()]
    any_spec = pl.BlockSpec(memory_space=pl.ANY)
    vmem = pl.BlockSpec(memory_space=pltpu.VMEM)
    V = pltpu.VMEM
    scratch = [
        V((4, TOK, D), BF16),
        V((4, TOK, D), BF16),
        V((D, 2 * HD), BF16),
        V((HD, D), BF16),
        V((4, ROWS, 2, HD), BF16),
        V((NX * NZ, 32, 128), F32),
        V((NX * NZ, TOK, TOK), F32),
        V((32, 128), F32),
        V((2, NY * PADD, NX * KD * TOK), BF16),
        V((2, NX * KG * TOK, NY * PADY), BF16),
        V((2, NY * PADD, 1), F32),
        V((2, ROWS, NX * NZ * TOK), BF16),
        V((2, NX * NZ * TOK, ROWS), BF16),
        V((2, ROWS, 1), F32),
        V((2, ROWS, HD), F32),
        V((2, ROWS, HD), F32),
        V((2, ROWS, HD), F32),
        V((2, ROWS, HD), F32),
        V((2, 2, 2, ROWS, HD), F32),
        V((2, ROWS, 2 * HD), BF16),
        V((2, ROWS, 2 * HD), BF16),
        V((2, NCH, NX, KD, TOK, 128), BF16),
        V((2, NCH, NY, PADD, 128), BF16),
        V((2, NCH, NZ, BLK, H1), BF16),
        V((2, NCH, NX, NZ, TOK, H3), BF16),
        V((2, NCH, NY, BLK, H3), BF16),
        V((RING, NY, PADD, 128), BF16),
        V((RING, NY, BLK, H3), BF16),
        V((RING, 2, BLK, H1), BF16),
        V((NCH, 2, HD, H1), BF16),
        V((2, ROWS, HD), BF16),
        V((2, 2, ROWS, HD), BF16),
        V((DEEP, NZ, BLK, C1), BF16),
        V((RING, 2, BLK, C1), BF16),
        V((2, NCH, BLK, C1), BF16),
        V((2, NCH, 2, BLK, C1), BF16),
        V((RING, NY, PADY, 128), BF16),
        V((2, NCH, NY, PADY, 128), BF16),
        V((RING, NX, KG, TOK, 128), BF16),
        V((2, NCH, KG, TOK, 128), BF16),
        V((RING, NY, BLK, C3), BF16),
        V((2, NCH, NY, BLK, C3), BF16),
        V((RING, NX, NZ * TOK, C3), BF16),
        V((2, NCH, NZ * TOK, C3), BF16),
        V((DEEP, NZ, TOK, C3), BF16),
        V((RING, 2, TOK, C3), BF16),
        V((2, NCH, TOK, C3), BF16),
        V((2, NCH, 2, TOK, C3), BF16),
        pltpu.SemaphoreType.DMA((RING, KINDS)),
        pltpu.SemaphoreType.DMA((NCH, KINDS)),
        pltpu.SemaphoreType.DMA((8,)),
        pltpu.SemaphoreType.DMA((8,)),
        pltpu.SemaphoreType.DMA((8,)),
        pltpu.SemaphoreType.DMA((RING,)),
        pltpu.SemaphoreType.DMA((NCH, 2)),
        pltpu.SemaphoreType.DMA((NCH, 2)),
        pltpu.SemaphoreType.DMA((2,)),
        pltpu.SemaphoreType.DMA((2, 2)),
    ]
    flops = 4 * 2 * ROWS * D * HD * 3
    return pl.pallas_call(
        kernel,
        out_shape=jax.ShapeDtypeStruct((4, TOK, D), BF16),
        in_specs=[any_spec] * 4 + [vmem] * 2 + [any_spec] * 4 + [vmem] * len(consts),
        out_specs=any_spec,
        scratch_shapes=scratch,
        compiler_params=pltpu.CompilerParams(
            collective_id=0, has_side_effects=True, vmem_limit_bytes=63 * 2**20
        ),
        cost_estimate=pl.CostEstimate(flops=flops, bytes_accessed=16 * 2**20, transcendentals=0),
        name="relay_layers",
    )(xa, xb, na, nb, ids, probs, saved, wg, wu, wdn, *consts)


def per_device(
    held_a, held_b, new_a, new_b, expert_ids, route_probs, saved_gate_up, w_gate, w_up, w_down
):
    ids, probs = expert_ids[0].transpose(0, 2, 1), route_probs[0].transpose(0, 2, 1)
    saved = saved_gate_up[0]
    out = layers(
        held_a[0], held_b[0], new_a, new_b, ids, probs, saved, w_gate[0], w_up[0], w_down[0]
    )
    return out[0][None], out[1][None], out[2][None], out[3][None]


def solution(mesh):
    in_specs = (
        P("pipe", "expert", None),
        P("pipe", "expert", None),
        P("expert", None),
        P("expert", None),
        P("pipe", None, "expert", None),
        P("pipe", None, "expert", None),
        P("pipe", None, None, None, "expert"),
        P("pipe", None, "expert"),
        P("pipe", None, "expert"),
        P("pipe", "expert", None),
    )
    out_specs = (P("pipe", "expert", None),) * 4
    return jax.shard_map(
        per_device, mesh=mesh, in_specs=in_specs, out_specs=out_specs, check_vma=False
    )
```
